1024 devices in a mesh: dp: 8 (over x_hi, core), tensor: 16 (over z, x_lo), expert: 8 (over y).
Axes of the slice: x: 8 (x_hi: 4, x_lo: 2; x = x_hi * 2 + x_lo), y: 8, z: 8, core: 2. Of those that a mesh axis runs over, the one named last changes fastest.
Arguments:
- tokens: bfloat16 [8192, 3072], P(('dp', 'expert'), 'tensor'), may hold values from -6 to 6
- expert_ids: int32 [8192, 4], P(('dp', 'expert')), may hold values from 0 to 7, all different within a row; in each aligned block of 128 rows (0 to 127, 128 to 255, ...) at most 72 rows name the same one
- gate_raw: float32 [8192, 4], P(('dp', 'expert')), may hold values from 0.05 to 10, as said below
- w_gate: bfloat16 [8, 3072, 5376], P('expert', None, 'tensor'), may hold values from -0.109375 to 0.109375
- w_up: bfloat16 [8, 3072, 5376], P('expert', None, 'tensor'), may hold values from -0.109375 to 0.109375
- w_down: bfloat16 [8, 5376, 3072], P('expert', 'tensor'), may hold values from -0.078125 to 0.078125
Outputs:
- mixed: bfloat16 [8192, 3072], P(('dp', 'expert'), 'tensor')
- balance: float32 [], replicated
The draws below stay inside these ranges and needn't reach their ends.
Inputs may be any that keep to these rules, and one draw needn't show every extreme that they name: `expert_ids`: each row names 4 different experts; within each aligned block of 128 rows (the rows of one device) no expert is named by more than 72 rows, a bound that some block reaches. `gate_raw`: Positive.
All inputs are finite; a program needn't handle non-finite values.
Results may differ from the reference program's by a relative error of at most 0.024.
Values may be sent and summed in bfloat16 or wider, within the bound.
A program may use at most 64 MiB of HBM per device.

```python
import math
import jax
import jax.numpy as jnp
import numpy as np
from jax import lax

D = 3072
FF = 5376
TOK_DEV = 128
EXPERTS = 8
TOPK = 4
CAP = 72
TOKENS = 8192
N_DP = 8
N_TENSOR = 16
N_EXPERT = 8


def draw_gate_raw(key, part):
    key = jax.random.fold_in(key, 11)
    blocks = TOKENS // TOK_DEV
    device_pos = (jnp.arange(TOKENS, dtype=jnp.int32) // TOK_DEV).astype(jnp.float32) / float(blocks - 1)
    scale = 1.0 + 2.0 * device_pos
    base = jnp.exp(jax.random.uniform(key, (TOKENS, TOPK), jnp.float32, math.log(0.05), 0.0))
    return (base * scale[:, None]).astype(jnp.float32)


def levels(key, shape, pieces, low, high):
    level, own = 1.0, jax.random.fold_in(key, 6)
    for position, parts in pieces:
        steps = jnp.exp(jax.random.uniform(jax.random.fold_in(own, position), (parts,), jnp.float32, low / len(pieces), high / len(pieces)))
        level = level * jnp.repeat(steps, shape[position] // parts).reshape([-1 if axis == position else 1 for axis in range(len(shape))])
    return level


def routed_block(own_key, own, number, rows, amount, top, most, slope):
    sequence = jax.random.permutation(own_key, amount)
    heavy_load, usual = shares(amount, rows * top, most, slope, True), shares(amount, rows * top, most, slope, False)
    places = jnp.arange(amount)

    def named(tallies, turn):
        used = int((tallies > 0).sum())
        fixed = max(1, used // 4)
        shifted = fixed + (places - fixed + turn * (used - fixed)) % max(1, amount - fixed)
        return jnp.zeros((amount,), jnp.int32).at[sequence[jnp.where(places < fixed, places, shifted)]].set(jnp.asarray(tallies, jnp.int32))

    tallies = jnp.where(number % 4 == 0, named(heavy_load, number // 4), named(usual, number - number // 4 - 1))
    mixed = jax.random.permutation(jax.random.fold_in(own, 3), amount)
    source_of, sink = mixed[0:amount // 2 * 2:2], mixed[1:amount // 2 * 2:2]
    margin = jnp.minimum(tallies[source_of] - 1, most - tallies[sink]) // 2
    margin = jnp.where((source_of == sequence[0]) | (sink == sequence[0]) | (tallies[sink] == 0), 0, jnp.maximum(margin, 0))
    shifted = jax.random.randint(jax.random.fold_in(own, 4), (amount // 2,), 0, 1 << 20) % (margin + 1)
    tallies = tallies.at[source_of].add(-shifted).at[sink].add(shifted)
    labels = jnp.searchsorted(jnp.cumsum(tallies), jnp.arange(rows * top), side="right").astype(jnp.int32)
    grid = labels.reshape(top, rows).T
    grid = grid[jax.random.permutation(jax.random.fold_in(own, 1), rows)]
    turn = jax.random.randint(jax.random.fold_in(own, 2), (rows, 1), 0, top)
    return jnp.take_along_axis(grid, (jnp.arange(top)[None, :] + turn) % top, axis=1)


def shares(count, total, most, skew, full):
    weights = [(1 << 20) // math.isqrt(standing ** skew) + 1 for standing in range(1, count + 1)]
    largest = most if full else min(most, max(-(-total // count), total * weights[0] // sum(weights)))
    least = 1 if total - largest >= count - 1 else 0
    given, surplus = [largest] + [least] * (count - 1), total - largest - least * (count - 1)
    while surplus > 0:
        movable = [i for i in range(1, count) if given[i] < largest] or [i for i in range(1, count) if given[i] < most]
        pool, left = sum([weights[i] for i in movable]), surplus
        for i in movable:
            addition = min(most - given[i], max(1, left * weights[i] // pool), surplus)
            given[i] = given[i] + addition
            surplus = surplus - addition
    return np.array(given)


def gaussian(own_key, shape, spread, most, cuts=(), held_as=jnp.bfloat16):
    result = jax.random.normal(own_key, shape, jnp.float32) * spread
    if len(cuts) > 0:
        result = levels(own_key, shape, cuts, -0.22, 0.18) * result
    return jnp.clip(result, min=-most, max=most).astype(held_as)


def setup_inputs(seed: int = 0) -> dict:
    key_list = jax.random.split(jax.random.key(seed), 7)
    tokens = gaussian(key_list[0], (TOKENS, D), 1.0, 6.0, ((0, 64), (1, 16)))
    expert_ids_keys = jax.random.split(jax.random.fold_in(key_list[1], 1), TOKENS // TOK_DEV)
    expert_ids_turns = jax.random.permutation(jax.random.fold_in(key_list[1], 3), TOKENS // TOK_DEV)
    expert_ids = jax.vmap(lambda own, number: routed_block(jax.random.fold_in(key_list[1], 2), own, number, TOK_DEV, EXPERTS, TOPK, CAP, 2))(expert_ids_keys, expert_ids_turns).reshape((TOKENS, TOPK))
    gate_raw = draw_gate_raw(jax.random.fold_in(key_list[6], 71), 0)
    w_gate = gaussian(key_list[3], (EXPERTS, D, FF), D ** -0.5, 0.109375, ((0, 8), (2, 16)))
    w_up = gaussian(key_list[4], (EXPERTS, D, FF), D ** -0.5, 0.109375, ((0, 8), (2, 16)))
    w_down = gaussian(key_list[5], (EXPERTS, FF, D), FF ** -0.5, 0.078125, ((0, 8), (1, 16)))
    return {"tokens": tokens, "expert_ids": expert_ids, "gate_raw": gate_raw, "w_gate": w_gate, "w_up": w_up, "w_down": w_down}


def reference(tokens, expert_ids, gate_raw, w_gate, w_up, w_down):
    gate_norm = gate_raw / jnp.sum(gate_raw, axis=1, keepdims=True)
    flat_ids = expert_ids.reshape(-1).astype(jnp.int32)
    flat_gates = gate_norm.reshape(-1)
    flat_raw = gate_raw.reshape(-1)
    order = jnp.argsort(flat_ids, stable=True).astype(jnp.int32)
    one_hot = (flat_ids[:, None] == jnp.arange(EXPERTS, dtype=jnp.int32)[None, :])
    route_totals = jnp.sum(one_hot.astype(jnp.int32), axis=0)
    starts = (jnp.cumsum(route_totals) - route_totals).astype(jnp.int32)
    limit = CAP * N_DP * N_EXPERT
    padded = jnp.concatenate([order, jnp.zeros((limit,), jnp.int32)])
    block_width = FF // N_TENSOR

    def expert_step(total, expert):
        route_index = lax.dynamic_slice_in_dim(padded, starts[expert], limit).astype(jnp.int32)
        in_range = jnp.arange(limit, dtype=jnp.int32) < route_totals[expert]
        picked_rows = tokens[route_index // TOPK]
        gate_sum = jnp.dot(picked_rows, w_gate[expert], preferred_element_type=jnp.float32)
        up_sum = jnp.dot(picked_rows, w_up[expert], preferred_element_type=jnp.float32)
        hidden = (jax.nn.silu(gate_sum) * up_sum).astype(jnp.bfloat16)
        down_matrix = w_down[expert]

        def block_step(accum, block):
            hidden_part = lax.dynamic_slice_in_dim(hidden, block * block_width, block_width, 1)
            weight_part = lax.dynamic_slice_in_dim(down_matrix, block * block_width, block_width, 0)
            partial_sum = jnp.dot(hidden_part, weight_part, preferred_element_type=jnp.float32)
            rounded = lax.optimization_barrier(partial_sum.astype(jnp.bfloat16))
            return accum + rounded.astype(jnp.float32), None

        summed, _ = lax.scan(block_step, jnp.zeros((limit, D), jnp.float32), jnp.arange(N_TENSOR, dtype=jnp.int32))
        expert_out = lax.optimization_barrier(summed.astype(jnp.bfloat16)).astype(jnp.float32)
        weighting = jnp.where(in_range, flat_gates[route_index], 0.0)
        total = total.at[route_index // TOPK].add(weighting[:, None] * expert_out)
        return total, None

    total, _ = lax.scan(expert_step, jnp.zeros((TOKENS, D), jnp.float32), jnp.arange(EXPERTS, dtype=jnp.int32))
    mixed = total.astype(jnp.bfloat16)
    gate_mass = jnp.sum(one_hot.astype(jnp.float32) * flat_raw[:, None], axis=0)
    balance = EXPERTS * jnp.sum((gate_mass / TOKENS) ** 2)
    return mixed, balance
```

```python
import jax
import jax.numpy as jnp
from jax import lax
from jax.experimental import pallas as pl
from jax.experimental.pallas import tpu as pltpu
from jax.sharding import PartitionSpec as P

MESH = pl.DeviceIdType.MESH
F32 = jnp.float32
BF16 = jnp.bfloat16

NZ = 8
NY = 8
CAP = 72
PAD = 80
SRC = 4
HALF = SRC * CAP
ROWS = 2 * HALF
A = 160
BLO, B = A, 256
P1, OWN1 = HALF, HALF - A
P2 = ROWS - A


def remote(src, dst, send, recv, device):
    return pltpu.make_async_remote_copy(
        src_ref=src,
        dst_ref=dst,
        send_sem=send,
        recv_sem=recv,
        device_id=device,
        device_id_type=MESH,
    )


def kernel(
    tok, ids, raw, wg_hbm, wu_hbm, wd_hbm, out, bal,
    wg, wu, wd, tokx, wide, onehot, gates, slots, landing, gath, acc_g, acc_u, hid,
    sa, sb, ra, rb, xs, xr, cross_s, cross_r, back_s, back_r, mix_s, mix_r, mass, bfly,
    w_sem, tok_sem, y_send, y_recv, own_send, own_recv,
    g_send, g_recv, xf_send, xf_recv, r_send, r_recv, xs_send, xs_recv,
    cr_sem, bk_send, bk_recv, mx_sem, ms_send, ms_recv, bf_send, bf_recv,
):
    dp, ten, y = lax.axis_index("dp"), lax.axis_index("tensor"), lax.axis_index("expert")
    tokens, feat = tok.shape
    width = 2 * feat
    z, xl = ten // 2, lax.rem(ten, 2)
    turn = 1 - 2 * lax.rem(dp, 2)
    par = lax.rem(xl + y, 2)
    me_half = y // 2

    def at(steps):
        return lax.rem(z + turn * steps + 2 * NZ, NZ)

    partner = {"tensor": z * 2 + 1 - xl}
    ahead = {"tensor": at(1) * 2 + xl}
    behind = {"tensor": at(-1) * 2 + xl}

    def flip(bit):
        return dp + bit - 2 * bit * lax.rem(dp // bit, 2)

    loads = [
        pltpu.make_async_copy(src.at[0], dst, w_sem.at[i])
        for i, (src, dst) in enumerate(((wg_hbm, wg), (wu_hbm, wu), (wd_hbm, wd)))
    ]
    for load in loads:
        load.start()

    barrier = pltpu.get_barrier_semaphore()
    peers = [{"expert": lax.rem(y + i, NY)} for i in range(1, NY)]
    peers += [partner, ahead, behind] + [{"dp": flip(bit)} for bit in (1, 2, 4)]
    for peer in peers:
        pl.semaphore_signal(barrier, inc=1, device_id=peer, device_id_type=MESH)

    lane = lax.broadcasted_iota(jnp.int32, (tokens, 128), 1)
    ids_v, raw_v = ids[...], raw[...]
    norm_v = raw_v / jnp.sum(raw_v, axis=1, keepdims=True)
    named = jnp.zeros((tokens, 128), F32)
    weight = jnp.zeros((tokens, 128), F32)
    share = jnp.zeros((tokens, 128), F32)
    for k in range(ids.shape[1]):
        hit = ids_v[:, k : k + 1] == lane
        named = jnp.where(hit, 1.0, named)
        weight = jnp.where(hit, raw_v[:, k : k + 1], weight)
        share = jnp.where(hit, norm_v[:, k : k + 1], share)
    row = lax.broadcasted_iota(jnp.int32, (tokens, tokens), 0)
    col = lax.broadcasted_iota(jnp.int32, (tokens, tokens), 1)
    earlier = jnp.where(col < row, 1.0, 0.0).astype(BF16)
    rank = jnp.dot(earlier, named.astype(BF16), preferred_element_type=F32).astype(jnp.int32)
    slot_lane = lax.broadcasted_iota(jnp.int32, (tokens, PAD), 1)
    for j in range(SRC):
        lo, hi = slice(2 * j, 2 * j + 1), slice(2 * j + 1, 2 * j + 2)
        rank_j = jnp.where(par == 0, rank[:, lo], rank[:, hi])
        named_j = jnp.where(par == 0, named[:, lo], named[:, hi])
        gates[j] = jnp.where(par == 0, share[:, lo], share[:, hi])
        onehot[j] = jnp.where(slot_lane == rank_j, named_j, 0.0).astype(BF16)
    mass[pl.ds(y, 1)] = jnp.broadcast_to(jnp.sum(weight, axis=0, keepdims=True), (8, 128))[None]

    pl.semaphore_wait(barrier, len(peers))

    swap = remote(tok, tokx, tok_sem.at[0], tok_sem.at[1], partner)
    swap.start()
    place_r = lax.broadcasted_iota(jnp.int32, (feat, width), 0)
    place_c = lax.broadcasted_iota(jnp.int32, (feat, width), 1)
    mine = jnp.where(place_c == place_r + feat * xl, 1.0, 0.0).astype(BF16)
    other = jnp.where(place_c == place_r + feat * (1 - xl), 1.0, 0.0).astype(BF16)
    wide_v = jnp.dot(tok[...], mine, preferred_element_type=F32)
    swap.wait_recv()
    wide[...] = (wide_v + jnp.dot(tokx[...], other, preferred_element_type=F32)).astype(BF16)

    def to_expert(j):
        return remote(
            slots.at[j], landing.at[me_half], y_send.at[j], y_recv.at[me_half], {"expert": 2 * j + par}
        )

    def from_source(j):
        return remote(slots.at[j], landing.at[j], y_send.at[j], y_recv.at[j], {"expert": 2 * j + par})

    for j in range(SRC):
        block = lax.dot_general(
            onehot[j], wide[...], (((0,), (0,)), ((), ())), preferred_element_type=F32
        ).astype(BF16)
        slots[j] = block

        @pl.when(2 * j + par != y)
        def _():
            to_expert(j).start()

        @pl.when(2 * j + par == y)
        def _():
            landing[j] = block

    def mass_copy(i, slot):
        return remote(
            mass.at[y], mass.at[slot], ms_send.at[i], ms_recv.at[slot], {"expert": lax.rem(y + i + 1, NY)}
        )

    @pl.loop(0, NY - 1)
    def _(i):
        mass_copy(i, y).start()

    parts = []
    for j in range(SRC):

        @pl.when(2 * j + par != y)
        def _():
            from_source(j).wait_recv()

        parts.append(landing[j].astype(F32)[:CAP])
    gath[pl.ds(z, 1), pl.ds(0, HALF)] = jnp.concatenate(parts, axis=0).astype(BF16)[None]

    rows_a, rows_b = pl.ds(0, A), pl.ds(BLO, B)

    def ring(part, way, hop, chunk):
        rows = (rows_a, rows_b)[part]
        return remote(
            gath.at[chunk, rows], gath.at[chunk, rows],
            g_send.at[part, way, hop - 1], g_recv.at[part, way, hop - 1], (ahead, behind)[way],
        )

    def over_x(chunk):
        return remote(
            gath.at[chunk, rows_a], gath.at[chunk, pl.ds(P2, A)],
            xf_send.at[chunk], xf_recv.at[chunk], partner,
        )

    own = remote(
        gath.at[z, pl.ds(A, OWN1)], gath.at[z, pl.ds(P1, OWN1)], own_send, own_recv, partner
    )
    own.start()
    ring(0, 0, 1, z).start()
    ring(0, 1, 1, z).start()
    over_x(z).start()
    own.wait_recv()
    ring(1, 0, 1, z).start()
    ring(1, 1, 1, z).start()
    for load in loads:
        load.wait()
    acc_g[...] = jnp.zeros_like(acc_g)
    acc_u[...] = jnp.zeros_like(acc_u)

    def use(chunk):
        over_x(chunk).wait_recv()
        depth = pl.ds(pl.multiple_of(chunk * width, width), width)

        @pl.loop(0, 2)
        def _(i):
            rows = pl.ds(pl.multiple_of(i * HALF, HALF), HALF)
            block = gath[chunk, rows]
            acc_g[rows] += jnp.dot(block, wg[depth], preferred_element_type=F32)
            acc_u[rows] += jnp.dot(block, wu[depth], preferred_element_type=F32)

    @pl.loop(1, 5)
    def _(hop):
        from_back, from_front = at(-hop), at(hop)

        def arrive(part, way, most, chunk):
            @pl.when(hop <= most)
            def _():
                ring(part, way, hop, chunk).wait_recv()

                @pl.when(hop < most)
                def _():
                    ring(part, way, hop + 1, chunk).start()

                if part == 0:
                    over_x(chunk).start()

        arrive(0, 0, 4, from_back)
        arrive(0, 1, 3, from_front)

        @pl.loop(0, jnp.where(hop == 1, 1, 2))
        def _(i):
            use(at((hop - 1) * (2 * i - 1)))

        arrive(1, 0, 3, from_back)
        arrive(1, 1, 4, from_front)

    use(at(4))

    @pl.loop(0, 2)
    def _(i):
        rows = pl.ds(pl.multiple_of(i * HALF, HALF), HALF)
        gate = acc_g[rows]
        hid[rows] = (gate / (1.0 + jnp.exp(-gate)) * acc_u[rows]).astype(BF16)

    def product(rows, dest):
        cols = pl.ds(pl.multiple_of(dest * width, width), width)
        return jnp.dot(hid[rows], wd[:, cols], preferred_element_type=F32)

    def x_sum(dest):
        return remote(xs.at[dest], xr.at[dest], xs_send.at[dest], xs_recv.at[dest], partner)

    def give_x(i):
        away = (8 - i) // 2
        dest = at(away * (1 - 2 * lax.rem(i, 2)))
        xs[pl.ds(dest, 1)] = product(pl.ds(P2, A), dest).astype(BF16)[None]
        x_sum(dest).start()

    def sums(part, way, hop):
        slot = way * 4 + hop - 1
        src, dst = ((sa, ra), (sb, rb))[part]
        return remote(
            src.at[slot], dst.at[slot],
            r_send.at[part, way, hop - 1], r_recv.at[part, way, hop - 1], (ahead, behind)[way],
        )

    def pass_on(part, way, hop, most, first):
        dest = at((most + 1 - hop) * (1 - 2 * way))
        value = product((rows_a, rows_b)[part], dest)
        if part == 0:
            x_sum(dest).wait_recv()
            value = value + xr[dest].astype(F32)
        slot = way * 4 + hop - 1
        src, dst = ((sa, ra), (sb, rb))[part]
        if not first:
            sums(part, way, hop - 1).wait_recv()
            value = value + dst[slot - 1].astype(F32)
        src[pl.ds(slot, 1)] = value.astype(BF16)[None]
        sums(part, way, hop).start()

    @pl.loop(0, 2)
    def _(i):
        give_x(i)

    pass_on(1, 1, 1, 4, True)
    pass_on(1, 0, 1, 3, True)

    @pl.loop(2, 8)
    def _(i):
        give_x(i)

    pass_on(0, 0, 1, 4, True)
    pass_on(0, 1, 1, 3, True)

    @pl.loop(0, NY - 1)
    def _(i):
        mass_copy(i, lax.rem(y + i + 1, NY)).wait_recv()

    total = mass[0]
    for i in range(1, NY):
        total = total + mass[i]
    bfly[0] = total

    def pair_copy(i):
        return remote(
            bfly.at[2 * i], bfly.at[2 * i + 1], bf_send.at[i], bf_recv.at[i], {"dp": flip(2**i)}
        )

    pair_copy(0).start()

    @pl.loop(2, 5)
    def _(hop):
        pass_on(1, 1, hop, 4, False)

        @pl.when(hop <= 3)
        def _():
            pass_on(1, 0, hop, 3, False)

        pass_on(0, 0, hop, 4, False)

        @pl.when(hop <= 3)
        def _():
            pass_on(0, 1, hop, 3, False)

    for i in (1, 2):
        pair_copy(i - 1).wait_recv()
        bfly[2 * i] = bfly[2 * i - 2] + bfly[2 * i - 1]
        pair_copy(i).start()

    value_b = product(rows_b, z)
    sums(1, 0, 3).wait_recv()
    value_b = value_b + rb[2].astype(F32)
    sums(1, 1, 4).wait_recv()
    value_b = value_b + rb[7].astype(F32)
    cross_s[...] = value_b[OWN1:].astype(BF16)
    crossing = remote(cross_s, cross_r, cr_sem.at[0], cr_sem.at[1], partner)
    crossing.start()
    x_sum(z).wait_recv()
    value_a = product(rows_a, z) + xr[z].astype(F32)
    sums(0, 1, 3).wait_recv()
    value_a = value_a + ra[6].astype(F32)
    sums(0, 0, 4).wait_recv()
    value_a = value_a + ra[3].astype(F32)
    crossing.wait_recv()
    value_b = value_b[:OWN1] + cross_r[...].astype(F32)
    done = jnp.concatenate([value_a, value_b], axis=0)

    def to_source(j):
        return remote(
            back_s.at[j], back_r.at[me_half], bk_send.at[j], bk_recv.at[me_half], {"expert": 2 * j + par}
        )

    def from_expert(j):
        return remote(back_s.at[j], back_r.at[j], bk_send.at[j], bk_recv.at[j], {"expert": 2 * j + par})

    for j in range(SRC):
        block = jnp.concatenate(
            [done[j * CAP : (j + 1) * CAP], jnp.zeros((PAD - CAP, width), F32)], axis=0
        ).astype(BF16)
        back_s[j] = block

        @pl.when(2 * j + par != y)
        def _():
            to_source(j).start()

        @pl.when(2 * j + par == y)
        def _():
            back_r[j] = block

    mixed = jnp.zeros((tokens, width), F32)
    for j in range(SRC):

        @pl.when(2 * j + par != y)
        def _():
            from_expert(j).wait_recv()

        mixed = mixed + gates[j] * jnp.dot(onehot[j], back_r[j], preferred_element_type=F32)
    left, right = mixed[:, :feat], mixed[:, feat:]
    mix_s[...] = jnp.where(xl == 0, right, left).astype(BF16)
    mixing = remote(mix_s, mix_r, mx_sem.at[0], mx_sem.at[1], partner)
    mixing.start()

    pair_copy(2).wait_recv()
    every = (bfly[4] + bfly[5])[0:1] * (1.0 / (tokens * 64))
    bal[...] = NY * jnp.sum(every * every, axis=1, keepdims=True)

    swap.wait_send()
    own.wait_send()
    crossing.wait_send()
    for j in range(SRC):

        @pl.when(2 * j + par != y)
        def _():
            to_expert(j).wait_send()
            to_source(j).wait_send()

    @pl.loop(0, NY - 1)
    def _(i):
        mass_copy(i, y).wait_send()

    @pl.loop(0, NZ)
    def _(i):
        over_x(i).wait_send()
        x_sum(i).wait_send()

    for i in range(3):
        pair_copy(i).wait_send()

    @pl.loop(1, 5)
    def _(hop):
        ring(0, 0, hop, z).wait_send()
        ring(1, 1, hop, z).wait_send()
        sums(0, 0, hop).wait_send()
        sums(1, 1, hop).wait_send()

        @pl.when(hop <= 3)
        def _():
            ring(0, 1, hop, z).wait_send()
            ring(1, 0, hop, z).wait_send()
            sums(0, 1, hop).wait_send()
            sums(1, 0, hop).wait_send()

    mixing.wait_recv()
    out[...] = (jnp.where(xl == 0, left, right) + mix_r[...].astype(F32)).astype(BF16)
    mixing.wait_send()


def body(tokens, expert_ids, gate_raw, w_gate, w_up, w_down):
    count, feat = tokens.shape
    _, model, hidden = w_gate.shape
    width = 2 * feat
    vmem = pl.BlockSpec(memory_space=pltpu.VMEM)
    hbm = pl.BlockSpec(memory_space=pl.ANY)
    dma = pltpu.SemaphoreType.DMA
    mixed, balance = pl.pallas_call(
        kernel,
        out_shape=(
            jax.ShapeDtypeStruct((count, feat), BF16),
            jax.ShapeDtypeStruct((1, 1), F32),
        ),
        in_specs=[vmem, vmem, vmem, hbm, hbm, hbm],
        out_specs=(vmem, vmem),
        scratch_shapes=[
            pltpu.VMEM((model, hidden), BF16),
            pltpu.VMEM((model, hidden), BF16),
            pltpu.VMEM((hidden, model), BF16),
            pltpu.VMEM((count, feat), BF16),
            pltpu.VMEM((count, width), BF16),
            pltpu.VMEM((SRC, count, PAD), BF16),
            pltpu.VMEM((SRC, count, 1), F32),
            pltpu.VMEM((SRC, PAD, width), BF16),
            pltpu.VMEM((SRC, PAD, width), BF16),
            pltpu.VMEM((NZ, ROWS, width), BF16),
            pltpu.VMEM((ROWS, hidden), F32),
            pltpu.VMEM((ROWS, hidden), F32),
            pltpu.VMEM((ROWS, hidden), BF16),
            pltpu.VMEM((8, A, width), BF16),
            pltpu.VMEM((8, B, width), BF16),
            pltpu.VMEM((8, A, width), BF16),
            pltpu.VMEM((8, B, width), BF16),
            pltpu.VMEM((NZ, A, width), BF16),
            pltpu.VMEM((NZ, A, width), BF16),
            pltpu.VMEM((OWN1, width), BF16),
            pltpu.VMEM((OWN1, width), BF16),
            pltpu.VMEM((SRC, PAD, width), BF16),
            pltpu.VMEM((SRC, PAD, width), BF16),
            pltpu.VMEM((count, feat), BF16),
            pltpu.VMEM((count, feat), BF16),
            pltpu.VMEM((NY, 8, 128), F32),
            pltpu.VMEM((6, 8, 128), F32),
            dma((3,)),
            dma((2,)),
            dma((SRC,)),
            dma((SRC,)),
            dma(()),
            dma(()),
            dma((2, 2, 4)),
            dma((2, 2, 4)),
            dma((NZ,)),
            dma((NZ,)),
            dma((2, 2, 4)),
            dma((2, 2, 4)),
            dma((NZ,)),
            dma((NZ,)),
            dma((2,)),
            dma((SRC,)),
            dma((SRC,)),
            dma((2,)),
            dma((NY,)),
            dma((NY,)),
            dma((3,)),
            dma((3,)),
        ],
        compiler_params=pltpu.CompilerParams(
            collective_id=0, has_side_effects=True, vmem_limit_bytes=48 * 1024 * 1024
        ),
    )(tokens, expert_ids, gate_raw, w_gate, w_up, w_down)
    return (mixed, balance.reshape(()))


def solution(mesh):
    return jax.shard_map(
        body,
        mesh=mesh,
        in_specs=(
            P(("dp", "expert"), "tensor"),
            P(("dp", "expert"), None),
            P(("dp", "expert"), None),
            P("expert", None, "tensor"),
            P("expert", None, "tensor"),
            P("expert", "tensor", None),
        ),
        out_specs=(P(("dp", "expert"), "tensor"), P()),
        check_vma=False,
    )
```

```python
import jax
import jax.numpy as jnp
from jax import lax
from jax.experimental import pallas as pl
from jax.experimental.pallas import tpu as pltpu
from jax.sharding import PartitionSpec as P

MESH = pl.DeviceIdType.MESH
F32 = jnp.float32
BF16 = jnp.bfloat16

NZ = 8
NY = 8
CAP = 72
PAD = 80
SRC = 4
HALF = SRC * CAP
ROWS = 2 * HALF
A = 160
BLO, B = A, 256
P1, OWN1 = HALF, HALF - A
P2 = ROWS - A


def remote(src, dst, send, recv, device):
    return pltpu.make_async_remote_copy(
        src_ref=src,
        dst_ref=dst,
        send_sem=send,
        recv_sem=recv,
        device_id=device,
        device_id_type=MESH,
    )


def kernel(
    tok, ids, raw, wg_hbm, wu_hbm, wd_hbm, out, bal,
    wg, wu, wd, wide, onehot, gates, slots, landing, gath, acc_g, acc_u, hid,
    sa, sb, ra, rb, xs, xr, cross_s, cross_r, back_s, back_r, mix_s, mix_r, mass, bfly,
    w_sem, tok_sem, y_send, y_recv, own_send, own_recv,
    g_send, g_recv, xf_send, xf_recv, r_send, r_recv, xs_send, xs_recv,
    cr_sem, bk_send, bk_recv, mx_sem, ms_send, ms_recv, bf_send, bf_recv,
):
    dp, ten, y = lax.axis_index("dp"), lax.axis_index("tensor"), lax.axis_index("expert")
    feat, tokens = tok.shape
    width = 2 * feat
    z, xl = ten // 2, lax.rem(ten, 2)
    turn = 1 - 2 * lax.rem(dp, 2)
    par = lax.rem(xl + y, 2)
    me_half = y // 2

    def at(steps):
        return lax.rem(z + turn * steps + 2 * NZ, NZ)

    partner = {"tensor": z * 2 + 1 - xl}
    ahead = {"tensor": at(1) * 2 + xl}
    behind = {"tensor": at(-1) * 2 + xl}

    def flip(bit):
        return dp + bit - 2 * bit * lax.rem(dp // bit, 2)

    loads = [
        pltpu.make_async_copy(src.at[0], dst, w_sem.at[i])
        for i, (src, dst) in enumerate(((wg_hbm, wg), (wu_hbm, wu), (wd_hbm, wd)))
    ]
    for load in loads:
        load.start()

    barrier = pltpu.get_barrier_semaphore()
    peers = [{"expert": lax.rem(y + i, NY)} for i in range(1, NY)]
    peers += [partner, ahead, behind] + [{"dp": flip(bit)} for bit in (1, 2, 4)]
    for peer in peers:
        pl.semaphore_signal(barrier, inc=1, device_id=peer, device_id_type=MESH)

    expert = lax.broadcasted_iota(jnp.int32, (16, tokens), 0)
    ids_v, raw_v = ids[...], raw[...]
    norm_v = raw_v / jnp.sum(raw_v, axis=0, keepdims=True)
    named = jnp.zeros((16, tokens), F32)
    weight = jnp.zeros((16, tokens), F32)
    share = jnp.zeros((16, tokens), F32)
    for k in range(ids.shape[0]):
        hit = ids_v[k : k + 1] == expert
        named = jnp.where(hit, 1.0, named)
        weight = jnp.where(hit, raw_v[k : k + 1], weight)
        share = jnp.where(hit, norm_v[k : k + 1], share)
    row = lax.broadcasted_iota(jnp.int32, (tokens, tokens), 0)
    col = lax.broadcasted_iota(jnp.int32, (tokens, tokens), 1)
    earlier = jnp.where(row < col, 1.0, 0.0).astype(BF16)
    rank = jnp.dot(named.astype(BF16), earlier, preferred_element_type=F32).astype(jnp.int32)
    slot = lax.broadcasted_iota(jnp.int32, (PAD, tokens), 0)
    for j in range(SRC):
        lo, hi = slice(2 * j, 2 * j + 1), slice(2 * j + 1, 2 * j + 2)
        rank_j = jnp.where(par == 0, rank[lo], rank[hi])
        named_j = jnp.where(par == 0, named[lo], named[hi])
        gates[j] = jnp.where(par == 0, share[lo], share[hi])
        onehot[j] = jnp.where(slot == rank_j, named_j, 0.0).astype(BF16)
    mass[pl.ds(y, 1)] = jnp.broadcast_to(jnp.sum(weight[:NY], axis=1, keepdims=True), (NY, 128))[None]

    pl.semaphore_wait(barrier, len(peers))

    swap = remote(
        tok, wide.at[pl.ds(pl.multiple_of(xl * feat, feat), feat)], tok_sem.at[0], tok_sem.at[1], partner
    )
    swap.start()
    wide[pl.ds(pl.multiple_of(xl * feat, feat), feat)] = tok[...]
    swap.wait_recv()

    def to_expert(j):
        return remote(
            slots.at[j], landing.at[me_half], y_send.at[j], y_recv.at[me_half], {"expert": 2 * j + par}
        )

    def from_source(j):
        return remote(slots.at[j], landing.at[j], y_send.at[j], y_recv.at[j], {"expert": 2 * j + par})

    for j in range(SRC):
        block = lax.dot_general(
            onehot[j], wide[...], (((1,), (1,)), ((), ())), preferred_element_type=F32
        ).astype(BF16)
        slots[j] = block

        @pl.when(2 * j + par != y)
        def _():
            to_expert(j).start()

        @pl.when(2 * j + par == y)
        def _():
            landing[j] = block

    def mass_copy(i, slot):
        return remote(
            mass.at[y], mass.at[slot], ms_send.at[i], ms_recv.at[slot], {"expert": lax.rem(y + i + 1, NY)}
        )

    @pl.loop(0, NY - 1)
    def _(i):
        mass_copy(i, y).start()

    parts = []
    for j in range(SRC):

        @pl.when(2 * j + par != y)
        def _():
            from_source(j).wait_recv()

        parts.append(landing[j].astype(F32)[:CAP])
    gath[pl.ds(z, 1), pl.ds(0, HALF)] = jnp.concatenate(parts, axis=0).astype(BF16)[None]

    rows_a, rows_b = pl.ds(0, A), pl.ds(BLO, B)

    def ring(part, way, hop, chunk):
        rows = (rows_a, rows_b)[part]
        return remote(
            gath.at[chunk, rows], gath.at[chunk, rows],
            g_send.at[part, way, hop - 1], g_recv.at[part, way, hop - 1], (ahead, behind)[way],
        )

    def over_x(chunk):
        return remote(
            gath.at[chunk, rows_a], gath.at[chunk, pl.ds(P2, A)],
            xf_send.at[chunk], xf_recv.at[chunk], partner,
        )

    own = remote(
        gath.at[z, pl.ds(A, OWN1)], gath.at[z, pl.ds(P1, OWN1)], own_send, own_recv, partner
    )
    own.start()
    ring(0, 0, 1, z).start()
    ring(0, 1, 1, z).start()
    over_x(z).start()
    own.wait_recv()
    ring(1, 0, 1, z).start()
    ring(1, 1, 1, z).start()
    for load in loads:
        load.wait()
    acc_g[...] = jnp.zeros_like(acc_g)
    acc_u[...] = jnp.zeros_like(acc_u)

    def use(chunk):
        over_x(chunk).wait_recv()
        depth = pl.ds(pl.multiple_of(chunk * width, width), width)

        @pl.loop(0, 2)
        def _(i):
            rows = pl.ds(pl.multiple_of(i * HALF, HALF), HALF)
            block = gath[chunk, rows]
            for acc, weights in ((acc_g, wg), (acc_u, wu)):
                acc[rows] += lax.dot_general(
                    block, weights[:, depth], (((1,), (1,)), ((), ())), preferred_element_type=F32
                )

    @pl.loop(1, 5)
    def _(hop):
        from_back, from_front = at(-hop), at(hop)

        def arrive(part, way, most, chunk):
            @pl.when(hop <= most)
            def _():
                ring(part, way, hop, chunk).wait_recv()

                @pl.when(hop < most)
                def _():
                    ring(part, way, hop + 1, chunk).start()

                if part == 0:
                    over_x(chunk).start()

        arrive(0, 0, 4, from_back)
        arrive(0, 1, 3, from_front)

        @pl.loop(0, jnp.where(hop == 1, 1, 2))
        def _(i):
            use(at((hop - 1) * (2 * i - 1)))

        arrive(1, 0, 3, from_back)
        arrive(1, 1, 4, from_front)

    use(at(4))

    @pl.loop(0, 2)
    def _(i):
        rows = pl.ds(pl.multiple_of(i * HALF, HALF), HALF)
        gate = acc_g[rows]
        hid[rows] = (gate / (1.0 + jnp.exp(-gate)) * acc_u[rows]).astype(BF16)

    def product(rows, dest):
        cols = pl.ds(pl.multiple_of(dest * width, width), width)
        return jnp.dot(hid[rows], wd[:, cols], preferred_element_type=F32)

    def x_sum(dest):
        return remote(xs.at[dest], xr.at[dest], xs_send.at[dest], xs_recv.at[dest], partner)

    def give_x(i):
        away = (8 - i) // 2
        dest = at(away * (1 - 2 * lax.rem(i, 2)))
        xs[pl.ds(dest, 1)] = product(pl.ds(P2, A), dest).astype(BF16)[None]
        x_sum(dest).start()

    def sums(part, way, hop):
        slot = way * 4 + hop - 1
        src, dst = ((sa, ra), (sb, rb))[part]
        return remote(
            src.at[slot], dst.at[slot],
            r_send.at[part, way, hop - 1], r_recv.at[part, way, hop - 1], (ahead, behind)[way],
        )

    def pass_on(part, way, hop, most, first):
        dest = at((most + 1 - hop) * (1 - 2 * way))
        value = product((rows_a, rows_b)[part], dest)
        if part == 0:
            x_sum(dest).wait_recv()
            value = value + xr[dest].astype(F32)
        slot = way * 4 + hop - 1
        src, dst = ((sa, ra), (sb, rb))[part]
        if not first:
            sums(part, way, hop - 1).wait_recv()
            value = value + dst[slot - 1].astype(F32)
        src[pl.ds(slot, 1)] = value.astype(BF16)[None]
        sums(part, way, hop).start()

    @pl.loop(0, 2)
    def _(i):
        give_x(i)

    pass_on(1, 1, 1, 4, True)
    pass_on(1, 0, 1, 3, True)

    @pl.loop(2, 8)
    def _(i):
        give_x(i)

    pass_on(0, 0, 1, 4, True)
    pass_on(0, 1, 1, 3, True)

    @pl.loop(0, NY - 1)
    def _(i):
        mass_copy(i, lax.rem(y + i + 1, NY)).wait_recv()

    total = mass[0]
    for i in range(1, NY):
        total = total + mass[i]
    bfly[0] = total

    def pair_copy(i):
        return remote(
            bfly.at[2 * i], bfly.at[2 * i + 1], bf_send.at[i], bf_recv.at[i], {"dp": flip(2**i)}
        )

    pair_copy(0).start()

    @pl.loop(2, 5)
    def _(hop):
        pass_on(1, 1, hop, 4, False)

        @pl.when(hop <= 3)
        def _():
            pass_on(1, 0, hop, 3, False)

        pass_on(0, 0, hop, 4, False)

        @pl.when(hop <= 3)
        def _():
            pass_on(0, 1, hop, 3, False)

    for i in (1, 2):
        pair_copy(i - 1).wait_recv()
        bfly[2 * i] = bfly[2 * i - 2] + bfly[2 * i - 1]
        pair_copy(i).start()

    value_b = product(rows_b, z)
    sums(1, 0, 3).wait_recv()
    value_b = value_b + rb[2].astype(F32)
    sums(1, 1, 4).wait_recv()
    value_b = value_b + rb[7].astype(F32)
    cross_s[...] = value_b[OWN1:].astype(BF16)
    crossing = remote(cross_s, cross_r, cr_sem.at[0], cr_sem.at[1], partner)
    crossing.start()
    x_sum(z).wait_recv()
    value_a = product(rows_a, z) + xr[z].astype(F32)
    sums(0, 1, 3).wait_recv()
    value_a = value_a + ra[6].astype(F32)
    sums(0, 0, 4).wait_recv()
    value_a = value_a + ra[3].astype(F32)
    crossing.wait_recv()
    value_b = value_b[:OWN1] + cross_r[...].astype(F32)
    done = jnp.concatenate([value_a, value_b], axis=0)

    def to_source(j):
        return remote(
            back_s.at[j], back_r.at[me_half], bk_send.at[j], bk_recv.at[me_half], {"expert": 2 * j + par}
        )

    def from_expert(j):
        return remote(back_s.at[j], back_r.at[j], bk_send.at[j], bk_recv.at[j], {"expert": 2 * j + par})

    for j in range(SRC):
        block = jnp.concatenate(
            [done[j * CAP : (j + 1) * CAP], jnp.zeros((PAD - CAP, width), F32)], axis=0
        ).astype(BF16)
        back_s[j] = block

        @pl.when(2 * j + par != y)
        def _():
            to_source(j).start()

        @pl.when(2 * j + par == y)
        def _():
            back_r[j] = block

    mixed = jnp.zeros((width, tokens), F32)
    for j in range(SRC):

        @pl.when(2 * j + par != y)
        def _():
            from_expert(j).wait_recv()

        mixed = mixed + gates[j] * lax.dot_general(
            back_r[j], onehot[j], (((0,), (0,)), ((), ())), preferred_element_type=F32
        )
    left, right = mixed[:feat], mixed[feat:]
    mix_s[...] = jnp.where(xl == 0, right, left).astype(BF16)
    mixing = remote(mix_s, mix_r, mx_sem.at[0], mx_sem.at[1], partner)
    mixing.start()

    pair_copy(2).wait_recv()
    every = (bfly[4] + bfly[5]) * (1.0 / (tokens * 64))
    bal[...] = NY * jnp.sum(every * every, axis=0, keepdims=True)[:, :1]

    swap.wait_send()
    own.wait_send()
    crossing.wait_send()
    for j in range(SRC):

        @pl.when(2 * j + par != y)
        def _():
            to_expert(j).wait_send()
            to_source(j).wait_send()

    @pl.loop(0, NY - 1)
    def _(i):
        mass_copy(i, y).wait_send()

    @pl.loop(0, NZ)
    def _(i):
        over_x(i).wait_send()
        x_sum(i).wait_send()

    for i in range(3):
        pair_copy(i).wait_send()

    @pl.loop(1, 5)
    def _(hop):
        ring(0, 0, hop, z).wait_send()
        ring(1, 1, hop, z).wait_send()
        sums(0, 0, hop).wait_send()
        sums(1, 1, hop).wait_send()

        @pl.when(hop <= 3)
        def _():
            ring(0, 1, hop, z).wait_send()
            ring(1, 0, hop, z).wait_send()
            sums(0, 1, hop).wait_send()
            sums(1, 0, hop).wait_send()

    mixing.wait_recv()
    out[...] = (jnp.where(xl == 0, left, right) + mix_r[...].astype(F32)).astype(BF16)
    mixing.wait_send()


def body(tokens, expert_ids, gate_raw, w_gate, w_up, w_down):
    count, feat = tokens.shape
    _, model, hidden = w_gate.shape
    turned = [jnp.swapaxes(v, -1, -2) for v in (tokens, expert_ids, gate_raw, w_gate, w_up)]
    width = 2 * feat
    vmem = pl.BlockSpec(memory_space=pltpu.VMEM)
    hbm = pl.BlockSpec(memory_space=pl.ANY)
    dma = pltpu.SemaphoreType.DMA
    mixed, balance = pl.pallas_call(
        kernel,
        out_shape=(
            jax.ShapeDtypeStruct((feat, count), BF16),
            jax.ShapeDtypeStruct((1, 1), F32),
        ),
        in_specs=[vmem, vmem, vmem, hbm, hbm, hbm],
        out_specs=(vmem, vmem),
        scratch_shapes=[
            pltpu.VMEM((hidden, model), BF16),
            pltpu.VMEM((hidden, model), BF16),
            pltpu.VMEM((hidden, model), BF16),
            pltpu.VMEM((width, count), BF16),
            pltpu.VMEM((SRC, PAD, count), BF16),
            pltpu.VMEM((SRC, 1, count), F32),
            pltpu.VMEM((SRC, PAD, width), BF16),
            pltpu.VMEM((SRC, PAD, width), BF16),
            pltpu.VMEM((NZ, ROWS, width), BF16),
            pltpu.VMEM((ROWS, hidden), F32),
            pltpu.VMEM((ROWS, hidden), F32),
            pltpu.VMEM((ROWS, hidden), BF16),
            pltpu.VMEM((8, A, width), BF16),
            pltpu.VMEM((8, B, width), BF16),
            pltpu.VMEM((8, A, width), BF16),
            pltpu.VMEM((8, B, width), BF16),
            pltpu.VMEM((NZ, A, width), BF16),
            pltpu.VMEM((NZ, A, width), BF16),
            pltpu.VMEM((OWN1, width), BF16),
            pltpu.VMEM((OWN1, width), BF16),
            pltpu.VMEM((SRC, PAD, width), BF16),
            pltpu.VMEM((SRC, PAD, width), BF16),
            pltpu.VMEM((feat, count), BF16),
            pltpu.VMEM((feat, count), BF16),
            pltpu.VMEM((NY, 8, 128), F32),
            pltpu.VMEM((6, 8, 128), F32),
            dma((3,)),
            dma((2,)),
            dma((SRC,)),
            dma((SRC,)),
            dma(()),
            dma(()),
            dma((2, 2, 4)),
            dma((2, 2, 4)),
            dma((NZ,)),
            dma((NZ,)),
            dma((2, 2, 4)),
            dma((2, 2, 4)),
            dma((NZ,)),
            dma((NZ,)),
            dma((2,)),
            dma((SRC,)),
            dma((SRC,)),
            dma((2,)),
            dma((NY,)),
            dma((NY,)),
            dma((3,)),
            dma((3,)),
        ],
        compiler_params=pltpu.CompilerParams(
            collective_id=0, has_side_effects=True, vmem_limit_bytes=60 * 1024 * 1024
        ),
    )(*turned, w_down)
    return (mixed.T, balance.reshape(()))


def solution(mesh):
    return jax.shard_map(
        body,
        mesh=mesh,
        in_specs=(
            P(("dp", "expert"), "tensor"),
            P(("dp", "expert"), None),
            P(("dp", "expert"), None),
            P("expert", None, "tensor"),
            P("expert", None, "tensor"),
            P("expert", "tensor", None),
        ),
        out_specs=(P(("dp", "expert"), "tensor"), P()),
        check_vma=False,
    )
```

```python
import functools

import jax
import jax.numpy as jnp
from jax import lax
from jax.experimental import pallas as pl
from jax.experimental.pallas import tpu as pltpu
from jax.sharding import PartitionSpec as P

MESH = pl.DeviceIdType.MESH
F32 = jnp.float32
BF16 = jnp.bfloat16

NZ = 8
NY = 8
CAP = 72
PAD = 80
SRC = 4
PART = 2 * CAP
ROWS = 4 * PART
NEAR, FAR, FAR_X, NEAR_X = 0, PART, 2 * PART, 3 * PART
ROUND = (NEAR, FAR_X, FAR)
MOST = ((4, 3), (3, 4), (3, 4))


def remote(src, dst, send, recv, device):
    return pltpu.make_async_remote_copy(
        src_ref=src,
        dst_ref=dst,
        send_sem=send,
        recv_sem=recv,
        device_id=device,
        device_id_type=MESH,
    )


def kernel(
    tok, ids, raw, wg_hbm, wu_hbm, wd_hbm, out, bal,
    wg, wu, wd, wide, onehot, gates, slots, landing, gath, acc_g, acc_u, hid,
    sums_s, sums_r, xs, xr, cross_s, cross_r, back_s, back_r, mix_s, mix_r, mass, bfly,
    w_sem, tok_sem, y_send, y_recv, own_send, own_recv,
    g_send, g_recv, xf_send, xf_recv, r_send, r_recv, xs_send, xs_recv,
    cr_sem, bk_send, bk_recv, mx_sem, ms_send, ms_recv, bf_send, bf_recv,
):
    dp, ten, y = lax.axis_index("dp"), lax.axis_index("tensor"), lax.axis_index("expert")
    feat, tokens = tok.shape
    width = 2 * feat
    z, xl = ten // 2, lax.rem(ten, 2)
    turn = 1 - 2 * lax.rem(dp, 2)
    steps_y = (2 * xl, 1 - 3 * xl, 4 * xl - 1, 4 - 7 * xl)

    def at(steps):
        return lax.rem(z + turn * steps + 2 * NZ, NZ)

    partner = {"tensor": z * 2 + 1 - xl}
    ahead = {"tensor": at(1) * 2 + xl}
    behind = {"tensor": at(-1) * 2 + xl}

    def along_y(steps):
        return lax.rem(y + steps + NY, NY)

    def unless_own(j, act):
        if j == 0:
            pl.when(xl == 1)(act)
        else:
            act()

    def flip(bit):
        return dp + bit - 2 * bit * lax.rem(dp // bit, 2)

    loads = [
        pltpu.make_async_copy(src.at[0], dst, w_sem.at[i])
        for i, (src, dst) in enumerate(((wg_hbm, wg), (wu_hbm, wu), (wd_hbm, wd)))
    ]
    for load in loads:
        load.start()

    barrier = pltpu.get_barrier_semaphore()
    peers = [{"expert": lax.rem(y + i, NY)} for i in range(1, NY)]
    peers += [partner, ahead, behind] + [{"dp": flip(bit)} for bit in (1, 2, 4)]
    for peer in peers:
        pl.semaphore_signal(barrier, inc=1, device_id=peer, device_id_type=MESH)

    expert = lax.broadcasted_iota(jnp.int32, (16, tokens), 0)
    ids_v, raw_v = ids[...], raw[...]
    norm_v = raw_v / jnp.sum(raw_v, axis=0, keepdims=True)
    named = jnp.zeros((16, tokens), F32)
    weight = jnp.zeros((16, tokens), F32)
    share = jnp.zeros((16, tokens), F32)
    for k in range(ids.shape[0]):
        hit = ids_v[k : k + 1] == expert
        named = jnp.where(hit, 1.0, named)
        weight = jnp.where(hit, raw_v[k : k + 1], weight)
        share = jnp.where(hit, norm_v[k : k + 1], share)
    row = lax.broadcasted_iota(jnp.int32, (tokens, tokens), 0)
    col = lax.broadcasted_iota(jnp.int32, (tokens, tokens), 1)
    earlier = jnp.where(row < col, 1.0, 0.0).astype(BF16)
    rank = jnp.dot(named.astype(BF16), earlier, preferred_element_type=F32).astype(jnp.int32)
    rank = jnp.where(named > 0, rank, -1)
    slot = lax.broadcasted_iota(jnp.int32, (PAD, tokens), 0)
    for j in range(SRC):
        this = expert == along_y(steps_y[j])
        rank_j = jnp.sum(jnp.where(this, rank, 0), axis=0, keepdims=True)
        gates[j] = jnp.sum(jnp.where(this, share, 0.0), axis=0, keepdims=True)
        onehot[j] = jnp.where(slot == rank_j, 1.0, 0.0).astype(BF16)
    mass[pl.ds(y, 1)] = jnp.broadcast_to(jnp.sum(weight[:NY], axis=1, keepdims=True), (NY, 128))[None]

    pl.semaphore_wait(barrier, len(peers))

    swap = remote(
        tok, wide.at[pl.ds(pl.multiple_of(xl * feat, feat), feat)], tok_sem.at[0], tok_sem.at[1], partner
    )
    swap.start()
    wide[pl.ds(pl.multiple_of(xl * feat, feat), feat)] = tok[...]
    swap.wait_recv()

    def to_expert(j):
        return remote(
            slots.at[j], landing.at[j], y_send.at[j], y_recv.at[j], {"expert": along_y(steps_y[j])}
        )

    for j in range(SRC):
        slots[j] = lax.dot_general(
            onehot[j], wide[...], (((1,), (1,)), ((), ())), preferred_element_type=F32
        ).astype(BF16)
        unless_own(j, to_expert(j).start)

    @pl.when(xl == 0)
    def _():
        landing[0] = slots[0]

    def mass_copy(i, slot):
        return remote(
            mass.at[y], mass.at[slot], ms_send.at[i], ms_recv.at[slot], {"expert": lax.rem(y + i + 1, NY)}
        )

    def land(j, first):
        unless_own(j, to_expert(j).wait_recv)
        unless_own(j + 1, to_expert(j + 1).wait_recv)
        both = [landing[i].astype(F32)[:CAP] for i in (j, j + 1)]
        gath[pl.ds(z, 1), pl.ds(first, PART)] = jnp.concatenate(both, axis=0).astype(BF16)[None]

    def ring(part, way, hop, chunk):
        rows = pl.ds(ROUND[part], PART)
        return remote(
            gath.at[chunk, rows], gath.at[chunk, rows],
            g_send.at[part, way, hop - 1], g_recv.at[part, way, hop - 1], (ahead, behind)[way],
        )

    def over_x(chunk):
        return remote(
            gath.at[chunk, pl.ds(NEAR, PART)], gath.at[chunk, pl.ds(NEAR_X, PART)],
            xf_send.at[chunk], xf_recv.at[chunk], partner,
        )

    own = remote(
        gath.at[z, pl.ds(FAR, PART)], gath.at[z, pl.ds(FAR_X, PART)], own_send, own_recv, partner
    )
    land(0, NEAR)
    ring(0, 0, 1, z).start()
    ring(0, 1, 1, z).start()
    over_x(z).start()
    land(2, FAR)
    own.start()
    ring(2, 0, 1, z).start()
    ring(2, 1, 1, z).start()

    @pl.loop(0, NY - 1)
    def _(i):
        mass_copy(i, y).start()

    acc_g[...] = jnp.zeros_like(acc_g)
    acc_u[...] = jnp.zeros_like(acc_u)
    own.wait_recv()
    ring(1, 0, 1, z).start()
    ring(1, 1, 1, z).start()
    for load in loads:
        load.wait()

    def use(chunk, first, count):
        rows = pl.ds(first, count)
        depth = pl.ds(pl.multiple_of(chunk * width, width), width)
        for acc, weights in ((acc_g, wg), (acc_u, wu)):
            acc[rows] += lax.dot_general(
                gath[chunk, rows], weights[:, depth], (((1,), (1,)), ((), ())), preferred_element_type=F32
            )

    def activate(first, count):
        rows = pl.ds(first, count)
        gate = acc_g[rows]
        hid[rows] = (gate / (1.0 + jnp.exp(-gate)) * acc_u[rows]).astype(BF16)

    @pl.loop(1, 5)
    def _(hop):
        chunks = (at(-hop), at(hop))

        def arrive(part, way):
            @pl.when(hop <= MOST[part][way])
            def _():
                ring(part, way, hop, chunks[way]).wait_recv()

                @pl.when(hop < MOST[part][way])
                def _():
                    ring(part, way, hop + 1, chunks[way]).start()

                if part == 0:
                    over_x(chunks[way]).start()

        arrive(0, 0)
        arrive(0, 1)

        @pl.loop(0, jnp.where(hop == 1, 1, 2))
        def _(i):
            chunk = at((hop - 1) * (2 * i - 1))
            over_x(chunk).wait_recv()

            @pl.loop(0, 2)
            def _(half):
                use(chunk, pl.multiple_of(half * 2 * PART, 2 * PART), 2 * PART)

        for part in (2, 1):
            arrive(part, 0)
            arrive(part, 1)

    last = at(4)
    use(last, FAR, 2 * PART)
    activate(FAR, 2 * PART)

    def product(first, dest):
        cols = pl.ds(pl.multiple_of(dest * width, width), width)
        return jnp.dot(hid[pl.ds(first, PART)], wd[:, cols], preferred_element_type=F32)

    def x_sum(dest):
        return remote(xs.at[dest], xr.at[dest], xs_send.at[dest], xs_recv.at[dest], partner)

    def give_x(i):
        away = (8 - i) // 2
        dest = at(away * (1 - 2 * lax.rem(i, 2)))
        xs[pl.ds(dest, 1)] = product(NEAR_X, dest).astype(BF16)[None]
        x_sum(dest).start()

    def sums(part, way, hop):
        slot = way * 4 + hop - 1
        return remote(
            sums_s.at[part, slot], sums_r.at[part, slot],
            r_send.at[part, way, hop - 1], r_recv.at[part, way, hop - 1], (ahead, behind)[way],
        )

    def pass_on(part, way, hop, first=False):
        dest = at((MOST[part][way] + 1 - hop) * (1 - 2 * way))
        value = product(ROUND[part], dest)
        if part == 0:
            x_sum(dest).wait_recv()
            value = value + xr[dest].astype(F32)
        slot = way * 4 + hop - 1
        if not first:
            sums(part, way, hop - 1).wait_recv()
            value = value + sums_r[part, slot - 1].astype(F32)
        sums_s[part, pl.ds(slot, 1)] = value.astype(BF16)[None]
        sums(part, way, hop).start()

    for part in (1, 2):
        for way in (1, 0):
            pass_on(part, way, 1, True)
    over_x(last).wait_recv()
    for first in (NEAR_X, NEAR):
        use(last, first, PART)
        activate(first, PART)

    @pl.loop(0, 8)
    def _(i):
        give_x(i)

    pass_on(0, 0, 1, True)
    pass_on(0, 1, 1, True)

    @pl.loop(0, NY - 1)
    def _(i):
        mass_copy(i, lax.rem(y + i + 1, NY)).wait_recv()

    total = mass[0]
    for i in range(1, NY):
        total = total + mass[i]
    bfly[0] = total

    def pair_copy(i):
        return remote(
            bfly.at[2 * i], bfly.at[2 * i + 1], bf_send.at[i], bf_recv.at[i], {"dp": flip(2**i)}
        )

    pair_copy(0).start()

    @pl.loop(2, 5)
    def _(hop):
        for part in (1, 2, 0):
            for way in range(2):
                pl.when(hop <= MOST[part][way])(functools.partial(pass_on, part, way, hop))

        for i in (1, 2):

            @pl.when(hop == i + 2)
            def _(i=i):
                pair_copy(i - 1).wait_recv()
                bfly[2 * i] = bfly[2 * i - 2] + bfly[2 * i - 1]
                pair_copy(i).start()

    def total_of(part):
        value = product(ROUND[part], z)
        for way in range(2):
            most = MOST[part][way]
            sums(part, way, most).wait_recv()
            value = value + sums_r[part, way * 4 + most - 1].astype(F32)
        return value

    cross_s[...] = total_of(1).astype(BF16)
    crossing = remote(cross_s, cross_r, cr_sem.at[0], cr_sem.at[1], partner)
    crossing.start()

    def to_source(j):
        return remote(
            back_s.at[j], back_r.at[j], bk_send.at[j], bk_recv.at[j], {"expert": along_y(-steps_y[j])}
        )

    def give_back(done, j):
        for i in range(2):
            back_s[j + i] = jnp.concatenate(
                [done[i * CAP : (i + 1) * CAP], jnp.zeros((PAD - CAP, width), F32)], axis=0
            ).astype(BF16)
            unless_own(j + i, to_source(j + i).start)

    x_sum(z).wait_recv()
    give_back(total_of(0) + xr[z].astype(F32), 0)

    @pl.when(xl == 0)
    def _():
        back_r[0] = back_s[0]

    far = total_of(2)
    crossing.wait_recv()
    give_back(far + cross_r[...].astype(F32), 2)

    mixed = jnp.zeros((width, tokens), F32)
    for j in range(SRC):
        unless_own(j, to_source(j).wait_recv)
        mixed = mixed + gates[j] * lax.dot_general(
            back_r[j], onehot[j], (((0,), (0,)), ((), ())), preferred_element_type=F32
        )
    left, right = mixed[:feat], mixed[feat:]
    mix_s[...] = jnp.where(xl == 0, right, left).astype(BF16)
    mixing = remote(mix_s, mix_r, mx_sem.at[0], mx_sem.at[1], partner)
    mixing.start()

    pair_copy(2).wait_recv()
    every = (bfly[4] + bfly[5]) * (1.0 / (tokens * 64))
    bal[...] = NY * jnp.sum(every * every, axis=0, keepdims=True)[:, :1]

    swap.wait_send()
    own.wait_send()
    crossing.wait_send()
    for j in range(SRC):
        unless_own(j, to_expert(j).wait_send)
        unless_own(j, to_source(j).wait_send)

    @pl.loop(0, NY - 1)
    def _(i):
        mass_copy(i, y).wait_send()

    @pl.loop(0, NZ)
    def _(i):
        over_x(i).wait_send()
        x_sum(i).wait_send()

    for i in range(3):
        pair_copy(i).wait_send()

    @pl.loop(1, 5)
    def _(hop):
        for part in range(3):
            for way in range(2):

                def sent(part=part, way=way):
                    ring(part, way, hop, z).wait_send()
                    sums(part, way, hop).wait_send()

                pl.when(hop <= MOST[part][way])(sent)

    mixing.wait_recv()
    out[...] = (jnp.where(xl == 0, left, right) + mix_r[...].astype(F32)).astype(BF16)
    mixing.wait_send()


def body(tokens, expert_ids, gate_raw, w_gate, w_up, w_down):
    count, feat = tokens.shape
    _, model, hidden = w_gate.shape
    turned = [jnp.swapaxes(v, -1, -2) for v in (tokens, expert_ids, gate_raw, w_gate, w_up)]
    width = 2 * feat
    vmem = pl.BlockSpec(memory_space=pltpu.VMEM)
    hbm = pl.BlockSpec(memory_space=pl.ANY)
    dma = pltpu.SemaphoreType.DMA
    mixed, balance = pl.pallas_call(
        kernel,
        out_shape=(
            jax.ShapeDtypeStruct((feat, count), BF16),
            jax.ShapeDtypeStruct((1, 1), F32),
        ),
        in_specs=[vmem, vmem, vmem, hbm, hbm, hbm],
        out_specs=(vmem, vmem),
        scratch_shapes=[
            pltpu.VMEM((hidden, model), BF16),
            pltpu.VMEM((hidden, model), BF16),
            pltpu.VMEM((hidden, model), BF16),
            pltpu.VMEM((width, count), BF16),
            pltpu.VMEM((SRC, PAD, count), BF16),
            pltpu.VMEM((SRC, 1, count), F32),
            pltpu.VMEM((SRC, PAD, width), BF16),
            pltpu.VMEM((SRC, PAD, width), BF16),
            pltpu.VMEM((NZ, ROWS, width), BF16),
            pltpu.VMEM((ROWS, hidden), F32),
            pltpu.VMEM((ROWS, hidden), F32),
            pltpu.VMEM((ROWS, hidden), BF16),
            pltpu.VMEM((3, 8, PART, width), BF16),
            pltpu.VMEM((3, 8, PART, width), BF16),
            pltpu.VMEM((NZ, PART, width), BF16),
            pltpu.VMEM((NZ, PART, width), BF16),
            pltpu.VMEM((PART, width), BF16),
            pltpu.VMEM((PART, width), BF16),
            pltpu.VMEM((SRC, PAD, width), BF16),
            pltpu.VMEM((SRC, PAD, width), BF16),
            pltpu.VMEM((feat, count), BF16),
            pltpu.VMEM((feat, count), BF16),
            pltpu.VMEM((NY, 8, 128), F32),
            pltpu.VMEM((6, 8, 128), F32),
            dma((3,)),
            dma((2,)),
            dma((SRC,)),
            dma((SRC,)),
            dma(()),
            dma(()),
            dma((3, 2, 4)),
            dma((3, 2, 4)),
            dma((NZ,)),
            dma((NZ,)),
            dma((3, 2, 4)),
            dma((3, 2, 4)),
            dma((NZ,)),
            dma((NZ,)),
            dma((2,)),
            dma((SRC,)),
            dma((SRC,)),
            dma((2,)),
            dma((NY,)),
            dma((NY,)),
            dma((3,)),
            dma((3,)),
        ],
        compiler_params=pltpu.CompilerParams(
            collective_id=0, has_side_effects=True, vmem_limit_bytes=60 * 1024 * 1024
        ),
    )(*turned, w_down)
    return (mixed.T, balance.reshape(()))


def solution(mesh):
    return jax.shard_map(
        body,
        mesh=mesh,
        in_specs=(
            P(("dp", "expert"), "tensor"),
            P(("dp", "expert"), None),
            P(("dp", "expert"), None),
            P("expert", None, "tensor"),
            P("expert", None, "tensor"),
            P("expert", "tensor", None),
        ),
        out_specs=(P(("dp", "expert"), "tensor"), P()),
        check_vma=False,
    )
```

```python
import functools

import jax
import jax.numpy as jnp
from jax import lax
from jax.experimental import pallas as pl
from jax.experimental.pallas import tpu as pltpu
from jax.sharding import PartitionSpec as P

MESH = pl.DeviceIdType.MESH
F32 = jnp.float32
BF16 = jnp.bfloat16

NZ = 8
NY = 8
CAP = 72
PAD = 80
SRC = 4
PART = 2 * CAP
HALF, ROWS = 2 * PART, 4 * PART
GATHER = ((PART, PART), (HALF, PART), (0, PART))
OVER_X = (HALF + PART, PART)
SUMS = ((128, 160), (HALF, 128), (0, 128))
SUMS_X = (HALF + 128, 160)
MOST = ((4, 3), (3, 4), (3, 4))


def remote(src, dst, send, recv, device):
    return pltpu.make_async_remote_copy(
        src_ref=src,
        dst_ref=dst,
        send_sem=send,
        recv_sem=recv,
        device_id=device,
        device_id_type=MESH,
    )


def kernel(
    tok_hbm, ids_hbm, raw_hbm, wg_hbm, wu_hbm, wd_hbm, out, bal,
    tok, ids, raw, wg, wu, wd, wide, onehot, gates, slots, landing, gath, acc_g, acc_u, hid,
    sums_as, sums_ar, sums_bs, sums_br, xs, xr, cross_s, cross_r, back_s, back_r, mix_s, mix_r, mass, bfly,
    in_sem, w_sem, tok_sem, y_send, y_recv, own_send, own_recv,
    g_send, g_recv, xf_send, xf_recv, r_send, r_recv, xs_send, xs_recv,
    cr_sem, bk_send, bk_recv, mx_sem, ms_send, ms_recv, bf_send, bf_recv,
):
    dp, ten, y = lax.axis_index("dp"), lax.axis_index("tensor"), lax.axis_index("expert")
    feat, tokens = tok_hbm.shape
    width = 2 * feat
    z, xl = ten // 2, lax.rem(ten, 2)
    turn = 1 - 2 * lax.rem(dp, 2)
    steps_y = (2 * xl, 1 - 3 * xl, 4 * xl - 1, 4 - 7 * xl)

    def at(steps):
        return lax.rem(z + turn * steps + 2 * NZ, NZ)

    partner = {"tensor": z * 2 + 1 - xl}
    ahead = {"tensor": at(1) * 2 + xl}
    behind = {"tensor": at(-1) * 2 + xl}

    def along_y(steps):
        return lax.rem(y + steps + NY, NY)

    def unless_own(j, act):
        if j == 0:
            pl.when(xl == 1)(act)
        else:
            act()

    def flip(bit):
        return dp + bit - 2 * bit * lax.rem(dp // bit, 2)

    small = [
        pltpu.make_async_copy(src, dst, in_sem.at[i])
        for i, (src, dst) in enumerate(((ids_hbm, ids), (raw_hbm, raw), (tok_hbm, tok)))
    ]
    for load in small:
        load.start()
    loads = [
        pltpu.make_async_copy(src.at[0], dst, w_sem.at[i])
        for i, (src, dst) in enumerate(((wg_hbm, wg), (wu_hbm, wu), (wd_hbm, wd)))
    ]
    barrier = pltpu.get_barrier_semaphore()
    peers = [{"expert": lax.rem(y + i, NY)} for i in range(1, NY)]
    peers += [partner, ahead, behind] + [{"dp": flip(bit)} for bit in (1, 2, 4)]
    for peer in peers:
        pl.semaphore_signal(barrier, inc=1, device_id=peer, device_id_type=MESH)
    for load in loads:
        load.start()
    for load in small:
        load.wait()

    expert = lax.broadcasted_iota(jnp.int32, (16, tokens), 0)
    ids_v, raw_v = ids[...], raw[...]
    norm_v = raw_v / jnp.sum(raw_v, axis=0, keepdims=True)
    named = jnp.zeros((16, tokens), F32)
    weight = jnp.zeros((16, tokens), F32)
    share = jnp.zeros((16, tokens), F32)
    for k in range(ids.shape[0]):
        hit = ids_v[k : k + 1] == expert
        named = jnp.where(hit, 1.0, named)
        weight = jnp.where(hit, raw_v[k : k + 1], weight)
        share = jnp.where(hit, norm_v[k : k + 1], share)
    row = lax.broadcasted_iota(jnp.int32, (tokens, tokens), 0)
    col = lax.broadcasted_iota(jnp.int32, (tokens, tokens), 1)
    earlier = jnp.where(row < col, 1.0, 0.0).astype(BF16)
    rank = jnp.dot(named.astype(BF16), earlier, preferred_element_type=F32).astype(jnp.int32)
    rank = jnp.where(named > 0, rank, -1)
    slot = lax.broadcasted_iota(jnp.int32, (PAD, tokens), 0)
    for j in range(SRC):
        this = expert == along_y(steps_y[j])
        rank_j = jnp.sum(jnp.where(this, rank, 0), axis=0, keepdims=True)
        gates[j] = jnp.sum(jnp.where(this, share, 0.0), axis=0, keepdims=True)
        onehot[j] = jnp.where(slot == rank_j, 1.0, 0.0).astype(BF16)
    mass[pl.ds(y, 1)] = jnp.broadcast_to(jnp.sum(weight[:NY], axis=1, keepdims=True), (NY, 128))[None]

    pl.semaphore_wait(barrier, len(peers))

    swap = remote(
        tok, wide.at[pl.ds(pl.multiple_of(xl * feat, feat), feat)], tok_sem.at[0], tok_sem.at[1], partner
    )
    swap.start()
    wide[pl.ds(pl.multiple_of(xl * feat, feat), feat)] = tok[...]
    swap.wait_recv()

    def to_expert(j):
        return remote(
            slots.at[j], landing.at[j], y_send.at[j], y_recv.at[j], {"expert": along_y(steps_y[j])}
        )

    for j in range(SRC):
        slots[j] = lax.dot_general(
            onehot[j], wide[...], (((1,), (1,)), ((), ())), preferred_element_type=F32
        ).astype(BF16)
        unless_own(j, to_expert(j).start)

    @pl.when(xl == 0)
    def _():
        landing[0] = slots[0]

    def mass_copy(i, slot):
        return remote(
            mass.at[y], mass.at[slot], ms_send.at[i], ms_recv.at[slot], {"expert": lax.rem(y + i + 1, NY)}
        )

    def land(j, first):
        unless_own(j, to_expert(j).wait_recv)
        unless_own(j + 1, to_expert(j + 1).wait_recv)
        both = [landing[i].astype(F32)[:CAP] for i in (j, j + 1)]
        gath[pl.ds(z, 1), pl.ds(first, PART)] = jnp.concatenate(both, axis=0).astype(BF16)[None]

    def ring(part, way, hop, chunk):
        rows = pl.ds(*GATHER[part])
        return remote(
            gath.at[chunk, rows], gath.at[chunk, rows],
            g_send.at[part, way, hop - 1], g_recv.at[part, way, hop - 1], (ahead, behind)[way],
        )

    def over_x(chunk):
        return remote(
            gath.at[chunk, pl.ds(*GATHER[0])], gath.at[chunk, pl.ds(*OVER_X)],
            xf_send.at[chunk], xf_recv.at[chunk], partner,
        )

    own = remote(
        gath.at[z, pl.ds(*GATHER[2])], gath.at[z, pl.ds(*GATHER[1])], own_send, own_recv, partner
    )
    land(0, 0)
    own.start()
    ring(2, 0, 1, z).start()
    ring(2, 1, 1, z).start()
    land(2, PART)
    ring(0, 0, 1, z).start()
    ring(0, 1, 1, z).start()
    over_x(z).start()

    @pl.loop(0, NY - 1)
    def _(i):
        mass_copy(i, y).start()

    acc_g[...] = jnp.zeros_like(acc_g)
    acc_u[...] = jnp.zeros_like(acc_u)
    own.wait_recv()
    ring(1, 0, 1, z).start()
    ring(1, 1, 1, z).start()
    for load in loads:
        load.wait()

    def use(chunk, first, count):
        rows = pl.ds(first, count)
        depth = pl.ds(pl.multiple_of(chunk * width, width), width)
        for acc, weights in ((acc_g, wg), (acc_u, wu)):
            acc[rows] += lax.dot_general(
                gath[chunk, rows], weights[:, depth], (((1,), (1,)), ((), ())), preferred_element_type=F32
            )

    def activate(first, count):
        rows = pl.ds(first, count)
        gate = acc_g[rows]
        hid[rows] = (gate / (1.0 + jnp.exp(-gate)) * acc_u[rows]).astype(BF16)

    @pl.loop(1, 5)
    def _(hop):
        chunks = (at(-hop), at(hop))

        def arrive(part, way):
            @pl.when(hop <= MOST[part][way])
            def _():
                ring(part, way, hop, chunks[way]).wait_recv()

                @pl.when(hop < MOST[part][way])
                def _():
                    ring(part, way, hop + 1, chunks[way]).start()

                if part == 0:
                    over_x(chunks[way]).start()

        def use_whole(chunk):
            over_x(chunk).wait_recv()

            @pl.loop(0, 2)
            def _(half):
                use(chunk, pl.multiple_of(half * 2 * PART, 2 * PART), 2 * PART)

        arrive(2, 0)
        pl.when(hop < 4)(functools.partial(arrive, 2, 1))
        arrive(0, 0)
        arrive(0, 1)
        use_whole(at(1 - hop))
        arrive(1, 0)
        pl.when(hop < 4)(functools.partial(arrive, 1, 1))
        pl.when(hop > 1)(lambda: use_whole(at(hop - 1)))

    last = at(4)
    for part in (2, 1):
        ring(part, 1, 4, last).wait_recv()
        use(last, *GATHER[part])
        activate(*GATHER[part])

    def product(rows, dest):
        cols = pl.ds(pl.multiple_of(dest * width, width), width)
        return jnp.dot(hid[pl.ds(*rows)], wd[:, cols], preferred_element_type=F32)

    def x_sum(dest):
        return remote(xs.at[dest], xr.at[dest], xs_send.at[dest], xs_recv.at[dest], partner)

    def give_x(i):
        away = (8 - i) // 2
        dest = at(away * (1 - 2 * lax.rem(i, 2)))
        xs[pl.ds(dest, 1)] = product(SUMS_X, dest).astype(BF16)[None]
        x_sum(dest).start()

    def boxes(part):
        return (sums_as, sums_ar) if part == 0 else (sums_bs.at[part - 1], sums_br.at[part - 1])

    def sums(part, way, hop):
        out_buf, in_buf = boxes(part)
        slot = way * 4 + hop - 1
        return remote(
            out_buf.at[slot], in_buf.at[slot],
            r_send.at[part, way, hop - 1], r_recv.at[part, way, hop - 1], (ahead, behind)[way],
        )

    def pass_on(part, way, hop, first=False):
        dest = at((MOST[part][way] + 1 - hop) * (1 - 2 * way))
        value = product(SUMS[part], dest)
        if part == 0:
            x_sum(dest).wait_recv()
            value = value + xr[dest].astype(F32)
        slot = way * 4 + hop - 1
        if not first:
            sums(part, way, hop - 1).wait_recv()
            value = value + boxes(part)[1][slot - 1].astype(F32)
        boxes(part)[0][pl.ds(slot, 1)] = value.astype(BF16)[None]
        sums(part, way, hop).start()

    for part in (1, 2):
        for way in (1, 0):
            pass_on(part, way, 1, True)
    over_x(last).wait_recv()
    for rows in (OVER_X, GATHER[0]):
        use(last, *rows)
        activate(*rows)

    @pl.loop(0, 8)
    def _(i):
        give_x(i)

    pass_on(0, 0, 1, True)
    pass_on(0, 1, 1, True)

    @pl.loop(0, NY - 1)
    def _(i):
        mass_copy(i, lax.rem(y + i + 1, NY)).wait_recv()

    total = mass[0]
    for i in range(1, NY):
        total = total + mass[i]
    bfly[0] = total

    def pair_copy(i):
        return remote(
            bfly.at[2 * i], bfly.at[2 * i + 1], bf_send.at[i], bf_recv.at[i], {"dp": flip(2**i)}
        )

    pair_copy(0).start()

    @pl.loop(2, 5)
    def _(hop):
        for part in (1, 2, 0):
            for way in range(2):
                pl.when(hop <= MOST[part][way])(functools.partial(pass_on, part, way, hop))

        for i in (1, 2):

            @pl.when(hop == i + 2)
            def _(i=i):
                pair_copy(i - 1).wait_recv()
                bfly[2 * i] = bfly[2 * i - 2] + bfly[2 * i - 1]
                pair_copy(i).start()

    def total_of(part):
        value = product(SUMS[part], z)
        for way in range(2):
            most = MOST[part][way]
            sums(part, way, most).wait_recv()
            value = value + boxes(part)[1][way * 4 + most - 1].astype(F32)
        return value

    cross_s[...] = total_of(1).astype(BF16)
    crossing = remote(cross_s, cross_r, cr_sem.at[0], cr_sem.at[1], partner)
    crossing.start()

    def to_source(j):
        return remote(
            back_s.at[j], back_r.at[j], bk_send.at[j], bk_recv.at[j], {"expert": along_y(-steps_y[j])}
        )

    def give_back(done, j):
        for i in range(2):
            back_s[j + i] = jnp.concatenate(
                [done[i * CAP : (i + 1) * CAP], jnp.zeros((PAD - CAP, width), F32)], axis=0
            ).astype(BF16)
            unless_own(j + i, to_source(j + i).start)

    x_sum(z).wait_recv()
    after = total_of(0) + xr[z].astype(F32)
    give_back(after[PART - 128 :], 2)
    before = total_of(2)
    crossing.wait_recv()
    before = before + cross_r[...].astype(F32)
    give_back(jnp.concatenate([before, after[: PART - 128]], axis=0), 0)

    @pl.when(xl == 0)
    def _():
        back_r[0] = back_s[0]

    mixed = jnp.zeros((width, tokens), F32)
    for j in (2, 3, 0, 1):
        unless_own(j, to_source(j).wait_recv)
        mixed = mixed + gates[j] * lax.dot_general(
            back_r[j], onehot[j], (((0,), (0,)), ((), ())), preferred_element_type=F32
        )
    left, right = mixed[:feat], mixed[feat:]
    mix_s[...] = jnp.where(xl == 0, right, left).astype(BF16)
    mixing = remote(mix_s, mix_r, mx_sem.at[0], mx_sem.at[1], partner)
    mixing.start()

    pair_copy(2).wait_recv()
    every = (bfly[4] + bfly[5]) * (1.0 / (tokens * 64))
    bal[...] = NY * jnp.sum(every * every, axis=0, keepdims=True)[:, :1]

    swap.wait_send()
    own.wait_send()
    crossing.wait_send()
    for j in range(SRC):
        unless_own(j, to_expert(j).wait_send)
        unless_own(j, to_source(j).wait_send)

    @pl.loop(0, NY - 1)
    def _(i):
        mass_copy(i, y).wait_send()

    @pl.loop(0, NZ)
    def _(i):
        over_x(i).wait_send()
        x_sum(i).wait_send()

    for i in range(3):
        pair_copy(i).wait_send()

    @pl.loop(1, 5)
    def _(hop):
        for part in range(3):
            for way in range(2):

                def sent(part=part, way=way):
                    ring(part, way, hop, z).wait_send()
                    sums(part, way, hop).wait_send()

                pl.when(hop <= MOST[part][way])(sent)

    mixing.wait_recv()
    out[...] = (jnp.where(xl == 0, left, right) + mix_r[...].astype(F32)).astype(BF16)
    mixing.wait_send()


def body(tokens, expert_ids, gate_raw, w_gate, w_up, w_down):
    count, feat = tokens.shape
    _, model, hidden = w_gate.shape
    turned = [jnp.swapaxes(v, -1, -2) for v in (tokens, expert_ids, gate_raw, w_gate, w_up)]
    width = 2 * feat
    vmem = pl.BlockSpec(memory_space=pltpu.VMEM)
    hbm = pl.BlockSpec(memory_space=pl.ANY)
    dma = pltpu.SemaphoreType.DMA
    mixed, balance = pl.pallas_call(
        kernel,
        out_shape=(
            jax.ShapeDtypeStruct((feat, count), BF16),
            jax.ShapeDtypeStruct((1, 1), F32),
        ),
        in_specs=[hbm] * 6,
        out_specs=(vmem, vmem),
        scratch_shapes=[
            pltpu.VMEM((feat, count), BF16),
            pltpu.VMEM(turned[1].shape, jnp.int32),
            pltpu.VMEM(turned[2].shape, F32),
            pltpu.VMEM((hidden, model), BF16),
            pltpu.VMEM((hidden, model), BF16),
            pltpu.VMEM((hidden, model), BF16),
            pltpu.VMEM((width, count), BF16),
            pltpu.VMEM((SRC, PAD, count), BF16),
            pltpu.VMEM((SRC, 1, count), F32),
            pltpu.VMEM((SRC, PAD, width), BF16),
            pltpu.VMEM((SRC, PAD, width), BF16),
            pltpu.VMEM((NZ, ROWS, width), BF16),
            pltpu.VMEM((ROWS, hidden), F32),
            pltpu.VMEM((ROWS, hidden), F32),
            pltpu.VMEM((ROWS, hidden), BF16),
            pltpu.VMEM((8, 160, width), BF16),
            pltpu.VMEM((8, 160, width), BF16),
            pltpu.VMEM((2, 8, 128, width), BF16),
            pltpu.VMEM((2, 8, 128, width), BF16),
            pltpu.VMEM((NZ, 160, width), BF16),
            pltpu.VMEM((NZ, 160, width), BF16),
            pltpu.VMEM((128, width), BF16),
            pltpu.VMEM((128, width), BF16),
            pltpu.VMEM((SRC, PAD, width), BF16),
            pltpu.VMEM((SRC, PAD, width), BF16),
            pltpu.VMEM((feat, count), BF16),
            pltpu.VMEM((feat, count), BF16),
            pltpu.VMEM((NY, 8, 128), F32),
            pltpu.VMEM((6, 8, 128), F32),
            dma((3,)),
            dma((3,)),
            dma((2,)),
            dma((SRC,)),
            dma((SRC,)),
            dma(()),
            dma(()),
            dma((3, 2, 4)),
            dma((3, 2, 4)),
            dma((NZ,)),
            dma((NZ,)),
            dma((3, 2, 4)),
            dma((3, 2, 4)),
            dma((NZ,)),
            dma((NZ,)),
            dma((2,)),
            dma((SRC,)),
            dma((SRC,)),
            dma((2,)),
            dma((NY,)),
            dma((NY,)),
            dma((3,)),
            dma((3,)),
        ],
        compiler_params=pltpu.CompilerParams(
            collective_id=0, has_side_effects=True, vmem_limit_bytes=60 * 1024 * 1024
        ),
    )(*turned, w_down)
    return (mixed.T, balance.reshape(()))


def solution(mesh):
    return jax.shard_map(
        body,
        mesh=mesh,
        in_specs=(
            P(("dp", "expert"), "tensor"),
            P(("dp", "expert"), None),
            P(("dp", "expert"), None),
            P("expert", None, "tensor"),
            P("expert", None, "tensor"),
            P("expert", "tensor", None),
        ),
        out_specs=(P(("dp", "expert"), "tensor"), P()),
        check_vma=False,
    )
```

```python
import functools

import jax
import jax.numpy as jnp
from jax import lax
from jax.experimental import pallas as pl
from jax.experimental.pallas import tpu as pltpu
from jax.sharding import PartitionSpec as P

MESH = pl.DeviceIdType.MESH
F32 = jnp.float32
BF16 = jnp.bfloat16

NZ = 8
NY = 8
CAP = 72
PAD = 80
SRC = 4
PART = 2 * CAP
HALF, ROWS = 2 * PART, 4 * PART
PARTS = ((128, 160), (HALF, 128), (0, 128))
OVER_X = (HALF + 128, 160)
MOST = ((4, 3), (3, 4), (3, 4))


def remote(src, dst, send, recv, device):
    return pltpu.make_async_remote_copy(
        src_ref=src,
        dst_ref=dst,
        send_sem=send,
        recv_sem=recv,
        device_id=device,
        device_id_type=MESH,
    )


def kernel(
    tok_hbm, ids_hbm, raw_hbm, wg_hbm, wu_hbm, wd_hbm, out, bal,
    tok, ids, raw, wg, wu, wd, wide, onehot, gates, slots, landing, gath, acc_g, acc_u, hid,
    sums_as, sums_ar, sums_bs, sums_br, xs, xr, cross_s, cross_r, back_s, back_r, mix_s, mix_r, mass, bfly,
    in_sem, w_sem, tok_sem, y_send, y_recv, own_send, own_recv,
    g_send, g_recv, xf_send, xf_recv, r_send, r_recv, xs_send, xs_recv,
    cr_sem, bk_send, bk_recv, mx_sem, ms_send, ms_recv, bf_send, bf_recv,
):
    dp, ten, y = lax.axis_index("dp"), lax.axis_index("tensor"), lax.axis_index("expert")
    feat, tokens = tok_hbm.shape
    width = 2 * feat
    z, xl = ten // 2, lax.rem(ten, 2)
    turn = 1 - 2 * lax.rem(dp, 2)
    steps_y = (2 * xl, 1 - 3 * xl, 4 * xl - 1, 4 - 7 * xl)

    def at(steps):
        return lax.rem(z + turn * steps + 2 * NZ, NZ)

    partner = {"tensor": z * 2 + 1 - xl}
    ahead = {"tensor": at(1) * 2 + xl}
    behind = {"tensor": at(-1) * 2 + xl}

    def along_y(steps):
        return lax.rem(y + steps + NY, NY)

    def unless_own(j, act):
        if j == 0:
            pl.when(xl == 1)(act)
        else:
            act()

    def flip(bit):
        return dp + bit - 2 * bit * lax.rem(dp // bit, 2)

    small = [
        pltpu.make_async_copy(src, dst, in_sem.at[i])
        for i, (src, dst) in enumerate(((ids_hbm, ids), (raw_hbm, raw), (tok_hbm, tok)))
    ]
    for copy in small:
        copy.start()
    span = wg.shape[1] // 4

    def load(i, quarter):
        src, dst = ((wg_hbm, wg), (wu_hbm, wu), (wd_hbm, wd))[i]
        cols = pl.ds(quarter * span, span)
        return pltpu.make_async_copy(src.at[0, :, cols], dst.at[:, cols], w_sem.at[i, quarter])

    barrier = pltpu.get_barrier_semaphore()
    peers = [{"expert": lax.rem(y + i, NY)} for i in range(1, NY)]
    peers += [partner, ahead, behind] + [{"dp": flip(bit)} for bit in (1, 2, 4)]
    for peer in peers:
        pl.semaphore_signal(barrier, inc=1, device_id=peer, device_id_type=MESH)
    for i in range(3):
        for quarter in range(4):
            load(i, quarter).start()
    for copy in small:
        copy.wait()

    expert = lax.broadcasted_iota(jnp.int32, (16, tokens), 0)
    ids_v, raw_v = ids[...], raw[...]
    norm_v = raw_v / jnp.sum(raw_v, axis=0, keepdims=True)
    named = jnp.zeros((16, tokens), F32)
    weight = jnp.zeros((16, tokens), F32)
    share = jnp.zeros((16, tokens), F32)
    for k in range(ids.shape[0]):
        hit = ids_v[k : k + 1] == expert
        named = jnp.where(hit, 1.0, named)
        weight = jnp.where(hit, raw_v[k : k + 1], weight)
        share = jnp.where(hit, norm_v[k : k + 1], share)
    row = lax.broadcasted_iota(jnp.int32, (tokens, tokens), 0)
    col = lax.broadcasted_iota(jnp.int32, (tokens, tokens), 1)
    earlier = jnp.where(row < col, 1.0, 0.0).astype(BF16)
    rank = jnp.dot(named.astype(BF16), earlier, preferred_element_type=F32).astype(jnp.int32)
    rank = jnp.where(named > 0, rank, -1)
    slot = lax.broadcasted_iota(jnp.int32, (PAD, tokens), 0)
    for j in range(SRC):
        this = expert == along_y(steps_y[j])
        rank_j = jnp.sum(jnp.where(this, rank, 0), axis=0, keepdims=True)
        gates[j] = jnp.sum(jnp.where(this, share, 0.0), axis=0, keepdims=True)
        onehot[j] = jnp.where(slot == rank_j, 1.0, 0.0).astype(BF16)
    mass[pl.ds(y, 1)] = jnp.broadcast_to(jnp.sum(weight[:NY], axis=1, keepdims=True), (NY, 128))[None]

    pl.semaphore_wait(barrier, len(peers))

    swap = remote(
        tok, wide.at[pl.ds(pl.multiple_of(xl * feat, feat), feat)], tok_sem.at[0], tok_sem.at[1], partner
    )
    swap.start()
    wide[pl.ds(pl.multiple_of(xl * feat, feat), feat)] = tok[...]
    swap.wait_recv()

    def to_expert(j):
        return remote(
            slots.at[j], landing.at[j], y_send.at[j], y_recv.at[j], {"expert": along_y(steps_y[j])}
        )

    for j in range(SRC):
        slots[j] = lax.dot_general(
            onehot[j], wide[...], (((1,), (1,)), ((), ())), preferred_element_type=F32
        ).astype(BF16)
        unless_own(j, to_expert(j).start)

    @pl.when(xl == 0)
    def _():
        landing[0] = slots[0]

    def mass_copy(i, slot):
        return remote(
            mass.at[y], mass.at[slot], ms_send.at[i], ms_recv.at[slot], {"expert": lax.rem(y + i + 1, NY)}
        )

    def land(j, first):
        unless_own(j, to_expert(j).wait_recv)
        unless_own(j + 1, to_expert(j + 1).wait_recv)
        both = [landing[i].astype(F32)[:CAP] for i in (j, j + 1)]
        gath[pl.ds(z, 1), pl.ds(first, PART)] = jnp.concatenate(both, axis=0).astype(BF16)[None]

    def ring(part, way, hop, chunk):
        rows = pl.ds(*PARTS[part])
        return remote(
            gath.at[chunk, rows], gath.at[chunk, rows],
            g_send.at[part, way, hop - 1], g_recv.at[part, way, hop - 1], (ahead, behind)[way],
        )

    def over_x(chunk):
        return remote(
            gath.at[chunk, pl.ds(*PARTS[0])], gath.at[chunk, pl.ds(*OVER_X)],
            xf_send.at[chunk], xf_recv.at[chunk], partner,
        )

    own = remote(
        gath.at[z, pl.ds(*PARTS[2])], gath.at[z, pl.ds(*PARTS[1])], own_send, own_recv, partner
    )
    land(0, 0)
    own.start()
    ring(2, 0, 1, z).start()
    ring(2, 1, 1, z).start()
    land(2, PART)
    ring(0, 0, 1, z).start()
    ring(0, 1, 1, z).start()
    over_x(z).start()

    @pl.loop(0, NY - 1)
    def _(i):
        mass_copy(i, y).start()

    acc_g[...] = jnp.zeros_like(acc_g)
    acc_u[...] = jnp.zeros_like(acc_u)
    own.wait_recv()
    ring(1, 0, 1, z).start()
    ring(1, 1, 1, z).start()

    def use(chunk, first, count):
        rows = pl.ds(first, count)
        depth = pl.ds(pl.multiple_of(chunk * width, width), width)
        for acc, weights in ((acc_g, wg), (acc_u, wu)):
            acc[rows] += lax.dot_general(
                gath[chunk, rows], weights[:, depth], (((1,), (1,)), ((), ())), preferred_element_type=F32
            )

    def activate(first, count):
        rows = pl.ds(first, count)
        gate = acc_g[rows]
        hid[rows] = (gate / (1.0 + jnp.exp(-gate)) * acc_u[rows]).astype(BF16)

    @pl.loop(1, 5)
    def _(hop):
        chunks = (at(-hop), at(hop))

        def arrive(part, way):
            @pl.when(hop <= MOST[part][way])
            def _():
                ring(part, way, hop, chunks[way]).wait_recv()

                @pl.when(hop < MOST[part][way])
                def _():
                    ring(part, way, hop + 1, chunks[way]).start()

                if part == 0:
                    over_x(chunks[way]).start()

        def use_whole(chunk):
            over_x(chunk).wait_recv()

            @pl.loop(0, 2)
            def _(half):
                use(chunk, pl.multiple_of(half * 2 * PART, 2 * PART), 2 * PART)

        arrive(2, 0)
        pl.when(hop < 4)(functools.partial(arrive, 2, 1))
        arrive(0, 0)
        arrive(0, 1)

        @pl.when(hop == 1)
        def _():
            for quarter in range(4):
                load(0, quarter).wait()
                load(1, quarter).wait()

        use_whole(at(1 - hop))
        arrive(1, 0)
        pl.when(hop < 4)(functools.partial(arrive, 1, 1))
        pl.when(hop > 1)(lambda: use_whole(at(hop - 1)))

    for quarter in range(4):
        load(2, quarter).wait()
    last = at(4)
    for part in (2, 1):
        ring(part, 1, 4, last).wait_recv()
        use(last, *PARTS[part])
        activate(*PARTS[part])

    def product(rows, dest):
        cols = pl.ds(pl.multiple_of(dest * width, width), width)
        return jnp.dot(hid[pl.ds(*rows)], wd[:, cols], preferred_element_type=F32)

    def x_sum(dest):
        return remote(xs.at[dest], xr.at[dest], xs_send.at[dest], xs_recv.at[dest], partner)

    def give_x(i):
        away = (8 - i) // 2
        dest = at(away * (1 - 2 * lax.rem(i, 2)))
        xs[pl.ds(dest, 1)] = product(OVER_X, dest).astype(BF16)[None]
        x_sum(dest).start()

    def boxes(part):
        return (sums_as, sums_ar) if part == 0 else (sums_bs.at[part - 1], sums_br.at[part - 1])

    def sums(part, way, hop):
        out_buf, in_buf = boxes(part)
        slot = way * 4 + hop - 1
        return remote(
            out_buf.at[slot], in_buf.at[slot],
            r_send.at[part, way, hop - 1], r_recv.at[part, way, hop - 1], (ahead, behind)[way],
        )

    def pass_on(part, way, hop, first=False):
        dest = at((MOST[part][way] + 1 - hop) * (1 - 2 * way))
        value = product(PARTS[part], dest)
        if part == 0:
            x_sum(dest).wait_recv()
            value = value + xr[dest].astype(F32)
        slot = way * 4 + hop - 1
        if not first:
            sums(part, way, hop - 1).wait_recv()
            value = value + boxes(part)[1][slot - 1].astype(F32)
        boxes(part)[0][pl.ds(slot, 1)] = value.astype(BF16)[None]
        sums(part, way, hop).start()

    for part in (1, 2):
        for way in (1, 0):
            pass_on(part, way, 1, True)
    over_x(last).wait_recv()
    for rows in (OVER_X, PARTS[0]):
        use(last, *rows)
        activate(*rows)

    @pl.loop(0, 8)
    def _(i):
        give_x(i)

    pass_on(0, 0, 1, True)
    pass_on(0, 1, 1, True)

    @pl.loop(0, NY - 1)
    def _(i):
        mass_copy(i, lax.rem(y + i + 1, NY)).wait_recv()

    total = mass[0]
    for i in range(1, NY):
        total = total + mass[i]
    bfly[0] = total

    def pair_copy(i):
        return remote(
            bfly.at[2 * i], bfly.at[2 * i + 1], bf_send.at[i], bf_recv.at[i], {"dp": flip(2**i)}
        )

    pair_copy(0).start()

    @pl.loop(2, 5)
    def _(hop):
        for part in (1, 2, 0):
            for way in range(2):
                pl.when(hop <= MOST[part][way])(functools.partial(pass_on, part, way, hop))

        for i in (1, 2):

            @pl.when(hop == i + 2)
            def _(i=i):
                pair_copy(i - 1).wait_recv()
                bfly[2 * i] = bfly[2 * i - 2] + bfly[2 * i - 1]
                pair_copy(i).start()

    swap.wait_send()
    own.wait_send()
    for j in range(SRC):
        unless_own(j, to_expert(j).wait_send)

    @pl.loop(0, NY - 1)
    def _(i):
        mass_copy(i, y).wait_send()

    @pl.loop(0, NZ)
    def _(i):
        over_x(i).wait_send()
        x_sum(i).wait_send()

    for i in range(2):
        pair_copy(i).wait_send()

    @pl.loop(1, 4)
    def _(hop):
        for part in range(3):
            for way in range(2):
                ring(part, way, hop, z).wait_send()
                sums(part, way, hop).wait_send()

    ring(0, 0, 4, z).wait_send()
    ring(1, 1, 4, z).wait_send()
    ring(2, 1, 4, z).wait_send()

    def total_of(part):
        value = product(PARTS[part], z)
        for way in range(2):
            most = MOST[part][way]
            sums(part, way, most).wait_recv()
            value = value + boxes(part)[1][way * 4 + most - 1].astype(F32)
        return value

    cross_s[...] = total_of(1).astype(BF16)
    crossing = remote(cross_s, cross_r, cr_sem.at[0], cr_sem.at[1], partner)
    crossing.start()

    def to_source(j):
        return remote(
            back_s.at[j], back_r.at[j], bk_send.at[j], bk_recv.at[j], {"expert": along_y(-steps_y[j])}
        )

    def give_back(done, j):
        for i in range(2):
            back_s[j + i] = jnp.concatenate(
                [done[i * CAP : (i + 1) * CAP], jnp.zeros((PAD - CAP, width), F32)], axis=0
            ).astype(BF16)
            unless_own(j + i, to_source(j + i).start)

    x_sum(z).wait_recv()
    after = total_of(0) + xr[z].astype(F32)
    give_back(after[PART - 128 :], 2)
    before = total_of(2)
    crossing.wait_recv()
    before = before + cross_r[...].astype(F32)
    give_back(jnp.concatenate([before, after[: PART - 128]], axis=0), 0)

    @pl.when(xl == 0)
    def _():
        back_r[0] = back_s[0]

    mixed = jnp.zeros((width, tokens), F32)
    for j in (2, 3, 0, 1):
        unless_own(j, to_source(j).wait_recv)
        mixed = mixed + gates[j] * lax.dot_general(
            back_r[j], onehot[j], (((0,), (0,)), ((), ())), preferred_element_type=F32
        )
    left, right = mixed[:feat], mixed[feat:]
    mix_s[...] = jnp.where(xl == 0, right, left).astype(BF16)
    mixing = remote(mix_s, mix_r, mx_sem.at[0], mx_sem.at[1], partner)
    mixing.start()

    pair_copy(2).wait_recv()
    every = (bfly[4] + bfly[5]) * (1.0 / (tokens * 64))
    bal[...] = NY * jnp.sum(every * every, axis=0, keepdims=True)[:, :1]

    crossing.wait_send()
    pair_copy(2).wait_send()
    sums(0, 0, 4).wait_send()
    sums(1, 1, 4).wait_send()
    sums(2, 1, 4).wait_send()
    for j in range(SRC):
        unless_own(j, to_source(j).wait_send)

    mixing.wait_recv()
    out[...] = (jnp.where(xl == 0, left, right) + mix_r[...].astype(F32)).astype(BF16)
    mixing.wait_send()


def body(tokens, expert_ids, gate_raw, w_gate, w_up, w_down):
    count, feat = tokens.shape
    _, model, hidden = w_gate.shape
    turned = [jnp.swapaxes(v, -1, -2) for v in (tokens, expert_ids, gate_raw, w_gate, w_up)]
    width = 2 * feat
    vmem = pl.BlockSpec(memory_space=pltpu.VMEM)
    hbm = pl.BlockSpec(memory_space=pl.ANY)
    dma = pltpu.SemaphoreType.DMA
    mixed, balance = pl.pallas_call(
        kernel,
        out_shape=(
            jax.ShapeDtypeStruct((feat, count), BF16),
            jax.ShapeDtypeStruct((1, 1), F32),
        ),
        in_specs=[hbm] * 6,
        out_specs=(vmem, vmem),
        scratch_shapes=[
            pltpu.VMEM((feat, count), BF16),
            pltpu.VMEM(turned[1].shape, jnp.int32),
            pltpu.VMEM(turned[2].shape, F32),
            pltpu.VMEM((hidden, model), BF16),
            pltpu.VMEM((hidden, model), BF16),
            pltpu.VMEM((hidden, model), BF16),
            pltpu.VMEM((width, count), BF16),
            pltpu.VMEM((SRC, PAD, count), BF16),
            pltpu.VMEM((SRC, 1, count), F32),
            pltpu.VMEM((SRC, PAD, width), BF16),
            pltpu.VMEM((SRC, PAD, width), BF16),
            pltpu.VMEM((NZ, ROWS, width), BF16),
            pltpu.VMEM((ROWS, hidden), F32),
            pltpu.VMEM((ROWS, hidden), F32),
            pltpu.VMEM((ROWS, hidden), BF16),
            pltpu.VMEM((8, 160, width), BF16),
            pltpu.VMEM((8, 160, width), BF16),
            pltpu.VMEM((2, 8, 128, width), BF16),
            pltpu.VMEM((2, 8, 128, width), BF16),
            pltpu.VMEM((NZ, 160, width), BF16),
            pltpu.VMEM((NZ, 160, width), BF16),
            pltpu.VMEM((128, width), BF16),
            pltpu.VMEM((128, width), BF16),
            pltpu.VMEM((SRC, PAD, width), BF16),
            pltpu.VMEM((SRC, PAD, width), BF16),
            pltpu.VMEM((feat, count), BF16),
            pltpu.VMEM((feat, count), BF16),
            pltpu.VMEM((NY, 8, 128), F32),
            pltpu.VMEM((6, 8, 128), F32),
            dma((3,)),
            dma((3, 4)),
            dma((2,)),
            dma((SRC,)),
            dma((SRC,)),
            dma(()),
            dma(()),
            dma((3, 2, 4)),
            dma((3, 2, 4)),
            dma((NZ,)),
            dma((NZ,)),
            dma((3, 2, 4)),
            dma((3, 2, 4)),
            dma((NZ,)),
            dma((NZ,)),
            dma((2,)),
            dma((SRC,)),
            dma((SRC,)),
            dma((2,)),
            dma((NY,)),
            dma((NY,)),
            dma((3,)),
            dma((3,)),
        ],
        compiler_params=pltpu.CompilerParams(
            collective_id=0, has_side_effects=True, vmem_limit_bytes=60 * 1024 * 1024
        ),
    )(*turned, w_down)
    return (mixed.T, balance.reshape(()))


def solution(mesh):
    return jax.shard_map(
        body,
        mesh=mesh,
        in_specs=(
            P(("dp", "expert"), "tensor"),
            P(("dp", "expert"), None),
            P(("dp", "expert"), None),
            P("expert", None, "tensor"),
            P("expert", None, "tensor"),
            P("expert", "tensor", None),
        ),
        out_specs=(P(("dp", "expert"), "tensor"), P()),
        check_vma=False,
    )
```

```python
import functools

import jax
import jax.numpy as jnp
from jax import lax
from jax.experimental import pallas as pl
from jax.experimental.pallas import tpu as pltpu
from jax.sharding import PartitionSpec as P

MESH = pl.DeviceIdType.MESH
F32 = jnp.float32
BF16 = jnp.bfloat16

NZ = 8
NY = 8
CAP = 72
PAD = 80
SRC = 4
PART = 2 * CAP
HALF, ROWS = 2 * PART, 4 * PART
GATHER = ((PART, PART), (HALF, PART), (0, PART))
OVER_X = (HALF + PART, PART)
SUMS = ((128, 160), (HALF, 128), (0, 128))
SUMS_X = (HALF + 128, 160)
MOST = ((4, 3), (3, 4), (3, 4))


def remote(src, dst, send, recv, device):
    return pltpu.make_async_remote_copy(
        src_ref=src,
        dst_ref=dst,
        send_sem=send,
        recv_sem=recv,
        device_id=device,
        device_id_type=MESH,
    )


def kernel(
    tok, ids, raw, wg_hbm, wu_hbm, wd_hbm, out, bal,
    wg, wu, wd, wide, onehot, gates, slots, landing, gath, acc_g, acc_u, hid,
    sums_as, sums_ar, sums_bs, sums_br, xs, xr, cross_s, cross_r, back_s, back_r, mix_s, mix_r, mass, bfly,
    w_sem, tok_sem, y_send, y_recv, own_send, own_recv,
    g_send, g_recv, xf_send, xf_recv, r_send, r_recv, xs_send, xs_recv,
    cr_sem, bk_send, bk_recv, mx_sem, ms_send, ms_recv, bf_send, bf_recv,
):
    dp, ten, y = lax.axis_index("dp"), lax.axis_index("tensor"), lax.axis_index("expert")
    feat, tokens = tok.shape
    width = 2 * feat
    z, xl = ten // 2, lax.rem(ten, 2)
    turn = 1 - 2 * lax.rem(dp, 2)
    steps_y = (2 * xl, 1 - 3 * xl, 4 * xl - 1, 4 - 7 * xl)

    def at(steps):
        return lax.rem(z + turn * steps + 2 * NZ, NZ)

    partner = {"tensor": z * 2 + 1 - xl}
    ahead = {"tensor": at(1) * 2 + xl}
    behind = {"tensor": at(-1) * 2 + xl}

    def along_y(steps):
        return lax.rem(y + steps + NY, NY)

    def unless_own(j, act):
        if j == 0:
            pl.when(xl == 1)(act)
        else:
            act()

    def flip(bit):
        return dp + bit - 2 * bit * lax.rem(dp // bit, 2)

    loads = [
        pltpu.make_async_copy(src.at[0], dst, w_sem.at[i])
        for i, (src, dst) in enumerate(((wg_hbm, wg), (wu_hbm, wu), (wd_hbm, wd)))
    ]
    for load in loads:
        load.start()

    barrier = pltpu.get_barrier_semaphore()
    peers = [{"expert": lax.rem(y + i, NY)} for i in range(1, NY)]
    peers += [partner, ahead, behind] + [{"dp": flip(bit)} for bit in (1, 2, 4)]
    for peer in peers:
        pl.semaphore_signal(barrier, inc=1, device_id=peer, device_id_type=MESH)

    expert = lax.broadcasted_iota(jnp.int32, (16, tokens), 0)
    ids_v, raw_v = ids[...], raw[...]
    norm_v = raw_v / jnp.sum(raw_v, axis=0, keepdims=True)
    named = jnp.zeros((16, tokens), F32)
    weight = jnp.zeros((16, tokens), F32)
    share = jnp.zeros((16, tokens), F32)
    for k in range(ids.shape[0]):
        hit = ids_v[k : k + 1] == expert
        named = jnp.where(hit, 1.0, named)
        weight = jnp.where(hit, raw_v[k : k + 1], weight)
        share = jnp.where(hit, norm_v[k : k + 1], share)
    row = lax.broadcasted_iota(jnp.int32, (tokens, tokens), 0)
    col = lax.broadcasted_iota(jnp.int32, (tokens, tokens), 1)
    earlier = jnp.where(row < col, 1.0, 0.0).astype(BF16)
    rank = jnp.dot(named.astype(BF16), earlier, preferred_element_type=F32).astype(jnp.int32)
    rank = jnp.where(named > 0, rank, -1)
    slot = lax.broadcasted_iota(jnp.int32, (PAD, tokens), 0)
    for j in range(SRC):
        this = expert == along_y(steps_y[j])
        rank_j = jnp.sum(jnp.where(this, rank, 0), axis=0, keepdims=True)
        gates[j] = jnp.sum(jnp.where(this, share, 0.0), axis=0, keepdims=True)
        onehot[j] = jnp.where(slot == rank_j, 1.0, 0.0).astype(BF16)
    mass[pl.ds(y, 1)] = jnp.broadcast_to(jnp.sum(weight[:NY], axis=1, keepdims=True), (NY, 128))[None]

    pl.semaphore_wait(barrier, len(peers))

    swap = remote(
        tok, wide.at[pl.ds(pl.multiple_of(xl * feat, feat), feat)], tok_sem.at[0], tok_sem.at[1], partner
    )
    swap.start()
    wide[pl.ds(pl.multiple_of(xl * feat, feat), feat)] = tok[...]
    swap.wait_recv()

    def to_expert(j):
        return remote(
            slots.at[j], landing.at[j], y_send.at[j], y_recv.at[j], {"expert": along_y(steps_y[j])}
        )

    for j in range(SRC):
        slots[j] = lax.dot_general(
            onehot[j], wide[...], (((1,), (1,)), ((), ())), preferred_element_type=F32
        ).astype(BF16)
        unless_own(j, to_expert(j).start)

    @pl.when(xl == 0)
    def _():
        landing[0] = slots[0]

    def mass_copy(i, slot):
        return remote(
            mass.at[y], mass.at[slot], ms_send.at[i], ms_recv.at[slot], {"expert": lax.rem(y + i + 1, NY)}
        )

    def land(j, first):
        unless_own(j, to_expert(j).wait_recv)
        unless_own(j + 1, to_expert(j + 1).wait_recv)
        both = [landing[i].astype(F32)[:CAP] for i in (j, j + 1)]
        gath[pl.ds(z, 1), pl.ds(first, PART)] = jnp.concatenate(both, axis=0).astype(BF16)[None]

    def ring(part, way, hop, chunk):
        rows = pl.ds(*GATHER[part])
        return remote(
            gath.at[chunk, rows], gath.at[chunk, rows],
            g_send.at[part, way, hop - 1], g_recv.at[part, way, hop - 1], (ahead, behind)[way],
        )

    def over_x(chunk):
        return remote(
            gath.at[chunk, pl.ds(*GATHER[0])], gath.at[chunk, pl.ds(*OVER_X)],
            xf_send.at[chunk], xf_recv.at[chunk], partner,
        )

    own = remote(
        gath.at[z, pl.ds(*GATHER[2])], gath.at[z, pl.ds(*GATHER[1])], own_send, own_recv, partner
    )
    land(0, 0)
    own.start()
    ring(2, 0, 1, z).start()
    ring(2, 1, 1, z).start()
    land(2, PART)
    ring(0, 0, 1, z).start()
    ring(0, 1, 1, z).start()
    over_x(z).start()

    @pl.loop(0, NY - 1)
    def _(i):
        mass_copy(i, y).start()

    acc_g[...] = jnp.zeros_like(acc_g)
    acc_u[...] = jnp.zeros_like(acc_u)
    own.wait_recv()
    ring(1, 0, 1, z).start()
    ring(1, 1, 1, z).start()
    for load in loads:
        load.wait()

    def use(chunk, first, count):
        rows = pl.ds(first, count)
        depth = pl.ds(pl.multiple_of(chunk * width, width), width)
        for acc, weights in ((acc_g, wg), (acc_u, wu)):
            acc[rows] += lax.dot_general(
                gath[chunk, rows], weights[:, depth], (((1,), (1,)), ((), ())), preferred_element_type=F32
            )

    def activate(first, count):
        rows = pl.ds(first, count)
        gate = acc_g[rows]
        hid[rows] = (gate / (1.0 + jnp.exp(-gate)) * acc_u[rows]).astype(BF16)

    @pl.loop(1, 5)
    def _(hop):
        chunks = (at(-hop), at(hop))

        def arrive(part, way):
            @pl.when(hop <= MOST[part][way])
            def _():
                ring(part, way, hop, chunks[way]).wait_recv()

                @pl.when(hop < MOST[part][way])
                def _():
                    ring(part, way, hop + 1, chunks[way]).start()

                if part == 0:
                    over_x(chunks[way]).start()

        def use_whole(chunk):
            over_x(chunk).wait_recv()

            @pl.loop(0, 2)
            def _(half):
                use(chunk, pl.multiple_of(half * 2 * PART, 2 * PART), 2 * PART)

        arrive(2, 0)
        pl.when(hop < 4)(functools.partial(arrive, 2, 1))
        arrive(0, 0)
        arrive(0, 1)
        use_whole(at(1 - hop))
        arrive(1, 0)
        pl.when(hop < 4)(functools.partial(arrive, 1, 1))
        pl.when(hop > 1)(lambda: use_whole(at(hop - 1)))

    last = at(4)
    for part in (2, 1):
        ring(part, 1, 4, last).wait_recv()
        use(last, *GATHER[part])
        activate(*GATHER[part])

    def product(rows, dest):
        cols = pl.ds(pl.multiple_of(dest * width, width), width)
        return jnp.dot(hid[pl.ds(*rows)], wd[:, cols], preferred_element_type=F32)

    def x_sum(dest):
        return remote(xs.at[dest], xr.at[dest], xs_send.at[dest], xs_recv.at[dest], partner)

    def give_x(i):
        away = (8 - i) // 2
        dest = at(away * (1 - 2 * lax.rem(i, 2)))
        xs[pl.ds(dest, 1)] = product(SUMS_X, dest).astype(BF16)[None]
        x_sum(dest).start()

    def boxes(part):
        return (sums_as, sums_ar) if part == 0 else (sums_bs.at[part - 1], sums_br.at[part - 1])

    def sums(part, way, hop):
        out_buf, in_buf = boxes(part)
        slot = way * 4 + hop - 1
        return remote(
            out_buf.at[slot], in_buf.at[slot],
            r_send.at[part, way, hop - 1], r_recv.at[part, way, hop - 1], (ahead, behind)[way],
        )

    def pass_on(part, way, hop, first=False):
        dest = at((MOST[part][way] + 1 - hop) * (1 - 2 * way))
        value = product(SUMS[part], dest)
        if part == 0:
            x_sum(dest).wait_recv()
            value = value + xr[dest].astype(F32)
        slot = way * 4 + hop - 1
        if not first:
            sums(part, way, hop - 1).wait_recv()
            value = value + boxes(part)[1][slot - 1].astype(F32)
        boxes(part)[0][pl.ds(slot, 1)] = value.astype(BF16)[None]
        sums(part, way, hop).start()

    for part in (1, 2):
        for way in (1, 0):
            pass_on(part, way, 1, True)
    over_x(last).wait_recv()
    for rows in (OVER_X, GATHER[0]):
        use(last, *rows)
        activate(*rows)

    @pl.loop(0, 8)
    def _(i):
        give_x(i)

    pass_on(0, 0, 1, True)
    pass_on(0, 1, 1, True)

    @pl.loop(0, NY - 1)
    def _(i):
        mass_copy(i, lax.rem(y + i + 1, NY)).wait_recv()

    total = mass[0]
    for i in range(1, NY):
        total = total + mass[i]
    bfly[0] = total

    def pair_copy(i):
        return remote(
            bfly.at[2 * i], bfly.at[2 * i + 1], bf_send.at[i], bf_recv.at[i], {"dp": flip(2**i)}
        )

    pair_copy(0).start()

    @pl.loop(2, 5)
    def _(hop):
        for part in (1, 2, 0):
            for way in range(2):
                pl.when(hop <= MOST[part][way])(functools.partial(pass_on, part, way, hop))

        for i in (1, 2):

            @pl.when(hop == i + 2)
            def _(i=i):
                pair_copy(i - 1).wait_recv()
                bfly[2 * i] = bfly[2 * i - 2] + bfly[2 * i - 1]
                pair_copy(i).start()

    def total_of(part):
        value = product(SUMS[part], z)
        for way in range(2):
            most = MOST[part][way]
            sums(part, way, most).wait_recv()
            value = value + boxes(part)[1][way * 4 + most - 1].astype(F32)
        return value

    cross_s[...] = total_of(1).astype(BF16)
    crossing = remote(cross_s, cross_r, cr_sem.at[0], cr_sem.at[1], partner)
    crossing.start()

    def to_source(j):
        return remote(
            back_s.at[j], back_r.at[j], bk_send.at[j], bk_recv.at[j], {"expert": along_y(-steps_y[j])}
        )

    def give_back(done, j):
        for i in range(2):
            back_s[j + i] = jnp.concatenate(
                [done[i * CAP : (i + 1) * CAP], jnp.zeros((PAD - CAP, width), F32)], axis=0
            ).astype(BF16)
            unless_own(j + i, to_source(j + i).start)

    x_sum(z).wait_recv()
    after = total_of(0) + xr[z].astype(F32)
    give_back(after[PART - 128 :], 2)
    before = total_of(2)
    crossing.wait_recv()
    before = before + cross_r[...].astype(F32)
    give_back(jnp.concatenate([before, after[: PART - 128]], axis=0), 0)

    @pl.when(xl == 0)
    def _():
        back_r[0] = back_s[0]

    mixed = jnp.zeros((width, tokens), F32)
    for j in (2, 3, 0, 1):
        unless_own(j, to_source(j).wait_recv)
        mixed = mixed + gates[j] * lax.dot_general(
            back_r[j], onehot[j], (((0,), (0,)), ((), ())), preferred_element_type=F32
        )
    left, right = mixed[:feat], mixed[feat:]
    mix_s[...] = jnp.where(xl == 0, right, left).astype(BF16)
    mixing = remote(mix_s, mix_r, mx_sem.at[0], mx_sem.at[1], partner)
    mixing.start()

    pair_copy(2).wait_recv()
    every = (bfly[4] + bfly[5]) * (1.0 / (tokens * 64))
    bal[...] = NY * jnp.sum(every * every, axis=0, keepdims=True)[:, :1]

    swap.wait_send()
    own.wait_send()
    crossing.wait_send()
    for j in range(SRC):
        unless_own(j, to_expert(j).wait_send)
        unless_own(j, to_source(j).wait_send)

    @pl.loop(0, NY - 1)
    def _(i):
        mass_copy(i, y).wait_send()

    @pl.loop(0, NZ)
    def _(i):
        over_x(i).wait_send()
        x_sum(i).wait_send()

    for i in range(3):
        pair_copy(i).wait_send()

    @pl.loop(1, 5)
    def _(hop):
        for part in range(3):
            for way in range(2):

                def sent(part=part, way=way):
                    ring(part, way, hop, z).wait_send()
                    sums(part, way, hop).wait_send()

                pl.when(hop <= MOST[part][way])(sent)

    mixing.wait_recv()
    out[...] = (jnp.where(xl == 0, left, right) + mix_r[...].astype(F32)).astype(BF16)
    mixing.wait_send()


def body(tokens, expert_ids, gate_raw, w_gate, w_up, w_down):
    count, feat = tokens.shape
    _, model, hidden = w_gate.shape
    turned = [jnp.swapaxes(v, -1, -2) for v in (tokens, expert_ids, gate_raw, w_gate, w_up)]
    width = 2 * feat
    vmem = pl.BlockSpec(memory_space=pltpu.VMEM)
    hbm = pl.BlockSpec(memory_space=pl.ANY)
    dma = pltpu.SemaphoreType.DMA
    mixed, balance = pl.pallas_call(
        kernel,
        out_shape=(
            jax.ShapeDtypeStruct((feat, count), BF16),
            jax.ShapeDtypeStruct((1, 1), F32),
        ),
        in_specs=[vmem, vmem, vmem, hbm, hbm, hbm],
        out_specs=(vmem, vmem),
        scratch_shapes=[
            pltpu.VMEM((hidden, model), BF16),
            pltpu.VMEM((hidden, model), BF16),
            pltpu.VMEM((hidden, model), BF16),
            pltpu.VMEM((width, count), BF16),
            pltpu.VMEM((SRC, PAD, count), BF16),
            pltpu.VMEM((SRC, 1, count), F32),
            pltpu.VMEM((SRC, PAD, width), BF16),
            pltpu.VMEM((SRC, PAD, width), BF16),
            pltpu.VMEM((NZ, ROWS, width), BF16),
            pltpu.VMEM((ROWS, hidden), F32),
            pltpu.VMEM((ROWS, hidden), F32),
            pltpu.VMEM((ROWS, hidden), BF16),
            pltpu.VMEM((8, 160, width), BF16),
            pltpu.VMEM((8, 160, width), BF16),
            pltpu.VMEM((2, 8, 128, width), BF16),
            pltpu.VMEM((2, 8, 128, width), BF16),
            pltpu.VMEM((NZ, 160, width), BF16),
            pltpu.VMEM((NZ, 160, width), BF16),
            pltpu.VMEM((128, width), BF16),
            pltpu.VMEM((128, width), BF16),
            pltpu.VMEM((SRC, PAD, width), BF16),
            pltpu.VMEM((SRC, PAD, width), BF16),
            pltpu.VMEM((feat, count), BF16),
            pltpu.VMEM((feat, count), BF16),
            pltpu.VMEM((NY, 8, 128), F32),
            pltpu.VMEM((6, 8, 128), F32),
            dma((3,)),
            dma((2,)),
            dma((SRC,)),
            dma((SRC,)),
            dma(()),
            dma(()),
            dma((3, 2, 4)),
            dma((3, 2, 4)),
            dma((NZ,)),
            dma((NZ,)),
            dma((3, 2, 4)),
            dma((3, 2, 4)),
            dma((NZ,)),
            dma((NZ,)),
            dma((2,)),
            dma((SRC,)),
            dma((SRC,)),
            dma((2,)),
            dma((NY,)),
            dma((NY,)),
            dma((3,)),
            dma((3,)),
        ],
        compiler_params=pltpu.CompilerParams(
            collective_id=0, has_side_effects=True, vmem_limit_bytes=52 * 1024 * 1024
        ),
    )(*turned, w_down)
    return (mixed.T, balance.reshape(()))


def solution(mesh):
    return jax.shard_map(
        body,
        mesh=mesh,
        in_specs=(
            P(("dp", "expert"), "tensor"),
            P(("dp", "expert"), None),
            P(("dp", "expert"), None),
            P("expert", None, "tensor"),
            P("expert", None, "tensor"),
            P("expert", "tensor", None),
        ),
        out_specs=(P(("dp", "expert"), "tensor"), P()),
        check_vma=False,
    )
```
